512 devices in a mesh: dp: 2 (over core), fsdp: 32 (over y, z_lo), tensor: 8 (over z_hi, x).
Axes of the slice: x: 4, y: 4, z: 16 (z_hi: 2, z_lo: 8; z = z_hi * 8 + z_lo), core: 2. Of those that a mesh axis runs over, the one named last changes fastest.
Arguments:
- tokens: bfloat16 [16384, 4096], P(('dp', 'fsdp', 'tensor')), may hold values from -40 to 40
- norm_gain: float32 [4096], replicated, may hold values from 0.5 to 1.5
- tile_values: bfloat16 [512, 128, 128], P(('fsdp', 'tensor')), may hold values from -0.25 to 0.25
- tile_rows: int32 [8, 64], P('tensor'), may hold values from 0 to 31, as said below
- tile_cols: int32 [8, 64], P('tensor'), may hold values from 0 to 13
- tile_counts: int32 [8, 32], P('tensor'), may hold values from 0 to 2, as said below
- grad_out: bfloat16 [16384, 14336], P(('dp', 'fsdp'), 'tensor'), may hold values from -3 to 3
Outputs:
- mixed: bfloat16 [16384, 14336], P(('dp', 'fsdp'), 'tensor')
- grad_x: bfloat16 [16384, 4096], P(('dp', 'fsdp', 'tensor'))
- grad_gain: float32 [4096], replicated
- grad_tiles: float32 [512, 128, 128], P(('fsdp', 'tensor'))
The draws below stay inside these ranges and needn't reach their ends.
Inputs may be any that keep to these rules, and one draw needn't show every extreme that they name: `tile_counts`: for each tensor index the counts over the 32 fsdp shards sum to 56, and some shard holds exactly 2. `tile_rows`: within one tensor index the (row, column) pairs of held slots are all different.
All inputs are finite; a program needn't handle non-finite values.
Results may differ from the reference program's by a relative error of at most 0.013.
Values may be sent and summed in bfloat16 or wider, within the bound.
A program may use at most 128 MiB of HBM per device.

```python
import jax
import jax.numpy as jnp
from jax import lax

TILE = 128
DW = 4096
FF = 14336
TOK_GRP = 256
TOKENS = 16384
FF_DEV = 1792
NNZ = 56
CAP = 2
N_DP = 2
N_FSDP = 32
N_TENSOR = 8


def tile_layout(key):
    row_tiles = DW // TILE
    col_tiles = FF // N_TENSOR // TILE
    slots_all = N_FSDP * CAP

    def one_shard(shard_key):
        key_one, key_two, key_three, key_four = jax.random.split(shard_key, 4)
        full_shard = jax.random.randint(key_one, (), 0, N_FSDP)
        shuffle = jax.random.permutation(key_two, slots_all)
        slot_shard = jnp.arange(slots_all) // CAP
        priority = jnp.where(slot_shard == full_shard, shuffle - slots_all, shuffle)
        slot_rank = jnp.argsort(jnp.argsort(priority))
        chosen = (slot_rank < NNZ).astype(jnp.int32)
        counts = jnp.sum(chosen.reshape(N_FSDP, CAP), axis=1).astype(jnp.int32)
        held = (jnp.arange(CAP)[None, :] < counts[:, None]).reshape(slots_all)
        positions = jax.random.permutation(key_three, row_tiles * col_tiles)[:NNZ]
        rank_held = jnp.clip(jnp.cumsum(held.astype(jnp.int32)) - 1, 0, NNZ - 1)
        unused_pos = jax.random.randint(key_four, (slots_all,), 0, row_tiles * col_tiles)
        position = jnp.where(held, positions[rank_held], unused_pos).astype(jnp.int32)
        return (position // col_tiles, position % col_tiles, counts)
    tensor_keys = jax.random.split(jax.random.fold_in(key, 7), N_TENSOR)
    return jax.vmap(one_shard)(tensor_keys)


def draw_tile_rows(key, part):
    return tile_layout(key)[0].astype(jnp.int32)


def draw_tile_cols(key, part):
    return tile_layout(key)[1].astype(jnp.int32)


def draw_tile_counts(key, part):
    return tile_layout(key)[2].astype(jnp.int32)


def draw_tokens(key, part):
    key_one, key_two, key_three = jax.random.split(jax.random.fold_in(key, 3), 3)
    row_scale = jnp.exp(jax.random.uniform(key_two, (TOKENS, 1), jnp.float32, -1.15, 1.15))
    col_scale = jnp.exp(jax.random.uniform(key_three, (1, DW), jnp.float32, -1.15, 1.15))
    base = jnp.clip(jax.random.normal(key_one, (TOKENS, DW), jnp.float32), -4.0, 4.0)
    return (base * row_scale * col_scale).astype(jnp.bfloat16)


def block_levels(own_key, extent, shards, least, high):
    loudness = 1.0
    for axis_at, blocks in shards:
        steps = jax.random.uniform(jax.random.fold_in(jax.random.fold_in(own_key, 6), axis_at), (blocks,), jnp.float32, least / len(shards), high / len(shards))
        loudness = loudness * jnp.repeat(jnp.exp(steps), extent[axis_at] // blocks).reshape((-1,) + (1,) * (len(extent) - 1 - axis_at))
    return loudness


def noise(stream_key, dims, spread, most, cuts=(), dtype=jnp.bfloat16):
    array = spread * jax.random.normal(stream_key, dims, jnp.float32)
    if cuts:
        array = array * block_levels(stream_key, dims, cuts, -0.22, 0.18)
    return jnp.clip(array, -most, most).astype(dtype)


def setup_inputs(seed: int = 0) -> dict:
    splits = jax.random.split(jax.random.key(seed), 8)
    return {
        "tokens": draw_tokens(jax.random.fold_in(splits[7], 71), 0),
        "norm_gain": jnp.clip(jax.random.uniform(splits[1], (DW,), jnp.float32, 0.5, 1.5), 0.5, 1.5),
        "tile_values": noise(splits[2], (N_FSDP * N_TENSOR * CAP, TILE, TILE), (DW // 8) ** -0.5, 0.25, ((0, 256),)),
        "tile_rows": draw_tile_rows(jax.random.fold_in(splits[7], 71), 0),
        "tile_cols": draw_tile_cols(jax.random.fold_in(splits[7], 71), 0),
        "tile_counts": draw_tile_counts(jax.random.fold_in(splits[7], 71), 0),
        "grad_out": noise(splits[6], (TOKENS, FF), 0.5, 3.0, ((0, 64), (1, 8))),
    }


def reference(tokens, norm_gain, tile_values, tile_rows, tile_cols, tile_counts, grad_out):
    local_float = tokens.astype(jnp.float32)
    inv_rms = lax.rsqrt(lax.optimization_barrier(jnp.mean(local_float * local_float, axis=1, keepdims=True)) + 1e-05)
    scaled = local_float * inv_rms
    normed = (scaled * norm_gain).astype(jnp.bfloat16)
    slots_all = N_FSDP * CAP
    row_tiles = DW // TILE
    col_tiles = FF_DEV // TILE
    groups = N_DP * N_FSDP
    values_by = tile_values.reshape(N_FSDP, N_TENSOR, CAP, TILE, TILE).transpose(1, 0, 2, 3, 4).reshape(N_TENSOR, slots_all, TILE, TILE)
    grad_by = grad_out.reshape(TOKENS, N_TENSOR, FF_DEV).transpose(1, 0, 2).reshape(N_TENSOR, groups, TOK_GRP, FF_DEV)
    x_groups = normed.astype(jnp.float32).reshape(groups, TOK_GRP, row_tiles, TILE)

    def per_shard(items):
        values, rows_list, cols_list, counts, grads = items
        held = (jnp.arange(CAP)[None, :] < counts[:, None]).reshape(slots_all)
        kept = jnp.where(held[:, None, None], values.astype(jnp.float32), jnp.float32(0.0))

        def per_group(pair):
            x_blocks, grad_rows = pair
            picked_x = jnp.take(x_blocks, rows_list, axis=1)
            product = jnp.einsum('tsk,skn->tsn', picked_x, kept)
            outputs = jnp.zeros((TOK_GRP, col_tiles, TILE), jnp.float32).at[:, cols_list].add(product)
            outputs = outputs.reshape(TOK_GRP, FF_DEV).astype(jnp.bfloat16)
            g_blocks = grad_rows.astype(jnp.float32).reshape(TOK_GRP, col_tiles, TILE)
            picked_g = jnp.take(g_blocks, cols_list, axis=1)
            backward = jnp.einsum('tsn,skn->tsk', picked_g, kept)
            partial_value = jnp.zeros((TOK_GRP, row_tiles, TILE), jnp.float32).at[:, rows_list].add(backward)
            partial_value = partial_value.reshape(TOK_GRP, DW).astype(jnp.bfloat16)
            terms = jnp.einsum('tsk,tsn->skn', picked_x, picked_g)
            return (outputs, partial_value, terms)
        outs_g, parts_g, terms_g = lax.map(per_group, (x_groups, grads))
        tile_grad = jnp.where(held[:, None, None], lax.optimization_barrier(jnp.sum(terms_g, axis=0)), jnp.float32(0.0))
        return (outs_g.reshape(TOKENS, FF_DEV), parts_g.reshape(TOKENS, DW), tile_grad)
    outs_all, partials, tile_grads = lax.map(per_shard, (values_by, tile_rows, tile_cols, tile_counts, grad_by))
    mixed = outs_all.transpose(1, 0, 2).reshape(TOKENS, FF)
    partials = lax.optimization_barrier(partials)
    input_grad = lax.optimization_barrier(jnp.sum(partials.astype(jnp.float32), axis=0))
    grad_gain = lax.optimization_barrier(jnp.sum(input_grad * scaled, axis=0))
    hidden_grad = input_grad * norm_gain
    grad_x = (inv_rms * (hidden_grad - scaled * lax.optimization_barrier(jnp.mean(hidden_grad * scaled, axis=1, keepdims=True)))).astype(jnp.bfloat16)
    grad_tiles = tile_grads.reshape(N_TENSOR, N_FSDP, CAP, TILE, TILE).transpose(1, 0, 2, 3, 4).reshape(N_FSDP * N_TENSOR * CAP, TILE, TILE)
    return (mixed, grad_x, grad_gain, grad_tiles)
```

```python
import functools

import jax
import jax.numpy as jnp
from jax import lax
from jax.experimental import pallas as pl
from jax.experimental.pallas import tpu as pltpu
from jax.sharding import PartitionSpec as P

MESH = pl.DeviceIdType.MESH
F32 = jnp.float32
BF16 = jnp.bfloat16
RT = 32
CT = 14
SLOTS = 64
NSEM = 128


class Net:
    def __init__(self, ssem, rsem, anyone):
        self.ssem, self.rsem, self.anyone = ssem, rsem, anyone
        self.sent = []

    def send(self, src, dst, device):
        i = len(self.sent)
        copy = pltpu.make_async_remote_copy(
            src_ref=src,
            dst_ref=dst,
            send_sem=self.ssem.at[i],
            recv_sem=self.rsem.at[i],
            device_id=device,
            device_id_type=MESH,
        )
        copy.start()
        self.sent.append(copy)
        return i

    def recv(self, i, ref):
        pltpu.make_async_remote_copy(
            src_ref=ref,
            dst_ref=ref,
            send_sem=self.ssem.at[i],
            recv_sem=self.rsem.at[i],
            device_id=self.anyone,
            device_id_type=MESH,
        ).wait_recv()


def lanes(i):
    return pl.ds(pl.multiple_of(i * 128, 128), 128)


def slot_tables(rows, cols, counts, zl, table):
    sub = lax.broadcasted_iota(jnp.int32, (SLOTS, SLOTS), 0)
    lane = lax.broadcasted_iota(jnp.int32, (SLOTS, SLOTS), 1)
    wide = lax.broadcasted_iota(jnp.int32, (SLOTS, 128), 1)
    slot = lax.broadcasted_iota(jnp.int32, (SLOTS, 1), 0)

    def over_lanes(mask, value):
        return jnp.sum(jnp.where(mask, value, 0), axis=1, keepdims=True)

    def over_slots(mask, value):
        return jnp.sum(jnp.where(mask, value, 0), axis=0, keepdims=True)

    def row(column_vector):
        return over_slots(sub == lane, column_vector)

    def put(k, vector):
        table[pl.ds(k, 1), :] = vector

    table[...] = jnp.zeros_like(table)
    row_of, col_of = over_lanes(sub == lane, rows), over_lanes(sub == lane, cols)
    shard = lax.broadcasted_iota(jnp.int32, (SLOTS, 32), 0) >> 1
    shard_lane = lax.broadcasted_iota(jnp.int32, (SLOTS, 32), 1)
    count = over_lanes(shard == shard_lane, counts)
    j = slot & 1
    held = count > j
    apart = ((slot >> 1) & 7) ^ zl
    place = ((apart & 1) << 2) | (apart & 2) | (apart >> 2)
    stored = j * 32 + (slot >> 4) * 8 + place
    for base, key, other in ((0, row_of, col_of), (5, col_of, row_of)):
        key = jnp.where(held, key, 64)
        order = key * 64 + slot
        rank = over_lanes(row(order) < order, 1)
        same = over_lanes((row(key) == key) & (lane < sub), 1)
        at = rank == wide
        for k, vector in ((0, stored), (1, other), (2, jnp.minimum(same, 1))):
            put(base + k, over_slots(at, vector))
        put(base + 3, jnp.maximum(over_slots(key <= wide, 1) - 1, 0))
        put(base + 4, jnp.minimum(over_slots(key == wide, 1), 1))
    at = stored == wide
    put(10, over_slots(at, row_of))
    put(11, over_slots(at, col_of))


def kernel(
    tok_hbm, gain, tv_hbm, rows, cols, counts, counts_s, go_hbm,
    mixed_hbm, gx_hbm, gg_hbm, gt_hbm,
    tok, go, gs, gt, x_all, scaled, inv, w, pb, pf, s, r, zs, zr, ig,
    dt, dr, e, es, yr, fs, fa, fr, tiles, mx, ox, table, sm,
    gp, gc, g1, gx4, gy, gh, gz, ga, ssem, rsem, lsem,
):
    d, f, t = lax.axis_index("dp"), lax.axis_index("fsdp"), lax.axis_index("tensor")
    h, x, y, zl = t // 4, lax.rem(t, 4), f // 8, lax.rem(f, 8)
    core = {"dp": 1 - d}
    other_half = {"tensor": lax.rem(t + 4, 8)}
    oc = lax.rem(t + 4, 8)

    def x_peer(k):
        return {"tensor": h * 4 + lax.rem(x + k, 4)}

    def y_peer(k):
        return {"fsdp": lax.rem(y + k, 4) * 8 + zl}

    z4 = {"fsdp": y * 8 + lax.rem(zl + 4, 8)}
    z2 = {"fsdp": f + 2 - 4 * lax.rem(zl // 2, 2)}
    z1 = {"fsdp": f + 1 - 2 * lax.rem(zl, 2)}
    partners = [core, other_half, z4, z2, z1]
    partners += [x_peer(k) for k in (1, 2, 3)] + [y_peer(k) for k in (1, 2, 3)]

    own_w = d * 32 + y * 8

    loads = [
        pltpu.make_async_copy(tok_hbm, tok, lsem.at[0]),
        pltpu.make_async_copy(tv_hbm.at[0], w.at[y * 8], lsem.at[1]),
        pltpu.make_async_copy(tv_hbm.at[1], w.at[32 + y * 8], lsem.at[2]),
        pltpu.make_async_copy(go_hbm, go, lsem.at[3]),
    ]
    for c in loads:
        c.start()
    barrier = pltpu.get_barrier_semaphore()
    for p in partners:
        pl.semaphore_signal(barrier, inc=1, device_id=p, device_id_type=MESH)

    loads[0].wait()

    def square(i, a):
        for u in range(4):
            v = tok[:, lanes(i * 4 + u)].astype(F32)
            a = a + v * v
        return a

    total = lax.fori_loop(0, RT // 4, square, jnp.zeros((32, 128), F32))
    inv_rms = lax.rsqrt(jnp.sum(total, axis=1, keepdims=True) * (1.0 / 4096.0) + 1e-05)
    inv[...] = jnp.broadcast_to(inv_rms, (32, 128))

    def norm(i, _):
        for u in range(4):
            rt = i * 4 + u
            v = tok[:, lanes(rt)].astype(F32) * inv[...]
            scaled[rt] = v
            x_all[t, rt] = (v * gain[pl.ds(rt, 1), :]).astype(BF16)
        return 0

    lax.fori_loop(0, RT // 4, norm, 0)
    loads[1].wait()
    loads[2].wait()
    pl.semaphore_wait(barrier, len(partners))

    net = Net(ssem, rsem, core)

    def w_at(base, lo, n):
        return w.at[pl.ds(base + lo, n)]

    def w_to_y(lo, n):
        return [net.send(w_at(own_w, lo, n), w_at(own_w, lo, n), y_peer(k)) for k in (1, 2, 3)]

    def x_chunk(c, q):
        return x_all.at[c, pl.ds(q * 8, 8)]

    wz = [net.send(w_at(own_w, 0, 1), w_at(own_w, 1, 1), z4)]
    wy = [w_to_y(0, 1)]
    xz = [net.send(x_chunk(t, 0), x_chunk(t, 0), other_half)]
    xown = [net.send(x_all.at[t], x_all.at[t], x_peer(k)) for k in (1, 2, 3)]
    xz.append(net.send(x_chunk(t, 1), x_chunk(t, 1), other_half))

    slot_tables(rows[...], cols[...], counts[...], zl, table)
    to_smem = pltpu.make_async_copy(table, sm, lsem.at[4])
    to_smem.start()

    net.recv(wz[0], w_at(own_w, 1, 1))
    wz.append(net.send(w_at(own_w, 0, 2), w_at(own_w, 2, 2), z2))
    wy.append(w_to_y(1, 1))

    loads[3].wait()
    for c in range(CT):
        v = go[:, c * 128 : (c + 1) * 128]
        gs[c] = v
        gt[c] = v.T

    net.recv(wz[1], w_at(own_w, 2, 2))
    wz.append(net.send(w_at(own_w, 0, 4), w_at(own_w, 4, 4), z1))
    wy.append(w_to_y(2, 2))
    xz.append(net.send(x_chunk(t, 2), x_chunk(t, 2), other_half))
    xz.append(net.send(x_chunk(t, 3), x_chunk(t, 3), other_half))

    xfwd = []

    def forward(q):
        net.recv(xz[q], x_chunk(oc, q))
        xfwd.append([net.send(x_chunk(oc, q), x_chunk(oc, q), x_peer(k)) for k in (1, 2, 3)])

    net.recv(wz[2], w_at(own_w, 4, 4))
    wy.append(w_to_y(4, 4))
    wc = [net.send(w_at(own_w, 1, 7), w_at(own_w, 1, 7), core)]
    forward(0)
    for k in (1, 2, 3):
        base = d * 32 + lax.rem(y + 4 - k, 4) * 8
        for ids, (lo, n) in zip(wy, ((0, 1), (1, 1), (2, 2), (4, 4))):
            net.recv(ids[k - 1], w_at(base, lo, n))
        wc.append(net.send(w_at(base, 0, 8), w_at(base, 0, 8), core))
    forward(1)
    other_w = (1 - d) * 32
    net.recv(wc[0], w_at(other_w + y * 8, 1, 7))
    for k in (1, 2, 3):
        net.recv(wc[k], w_at(other_w + lax.rem(y + 4 - k, 4) * 8, 0, 8))
    to_smem.wait()

    def back(b, acc):
        for u in range(4):
            i = b * 4 + u
            prod = lax.dot_general(gs[sm[1, i]], w[sm[0, i]], (((1,), (1,)), ((), ())), preferred_element_type=F32)
            acc = acc * sm[2, i].astype(F32) + prod
            pb[i] = acc.astype(BF16)
        return acc

    lax.fori_loop(0, SLOTS // 4, back, jnp.zeros((256, 128), F32))
    rs_other, rs_own = [], []

    def assemble(q):
        def one(rt, _):
            v = pb[sm[3, rt]].astype(F32) * sm[4, rt].astype(F32)
            s[:, rt] = v.astype(BF16).reshape(8, 32, 128)
            return 0

        lax.fori_loop(q * 8, q * 8 + 8, one, 0)

    def scatter(half, slot, q):
        ids = []
        for k in (1, 2, 3):
            to = half * 4 + lax.rem(x + k, 4)
            ids.append(net.send(s.at[to, pl.ds(q * 8, 8)], r.at[slot, k - 1, pl.ds(q * 8, 8)], x_peer(k)))
        return ids

    for q in range(4):
        assemble(q)
        rs_other.append(scatter(1 - h, 0, q))
    forward(2)
    for q in range(4):
        rs_own.append(scatter(h, 1, q))
    forward(3)

    zids = []

    def reduce_other(q):
        for k in (1, 2, 3):
            net.recv(rs_other[q][k - 1], r.at[0, k - 1, pl.ds(q * 8, 8)])

        def one(rt, _):
            v = s[oc, rt].astype(F32) + r[0, 0, rt].astype(F32)
            v = v + r[0, 1, rt].astype(F32) + r[0, 2, rt].astype(F32)
            zs[rt] = v.astype(BF16)
            return 0

        lax.fori_loop(q * 8, q * 8 + 8, one, 0)
        part = pl.ds(q * 8, 8)
        zids.append(net.send(zs.at[part], zr.at[part], other_half))

    for k in (1, 2, 3):
        net.recv(xown[k - 1], x_all.at[h * 4 + lax.rem(x + 4 - k, 4)])
    reduce_other(0)
    reduce_other(1)
    for k in (1, 2, 3):
        for q in range(4):
            net.recv(xfwd[q][k - 1], x_chunk((1 - h) * 4 + lax.rem(x + 4 - k, 4), q))

    def tile_grad(j, yy, out, cast):
        def one(q, _):
            p = j * 32 + yy * 8 + q
            xs = x_all[:, sm[10, p]].reshape(256, 128)
            out[yy * 8 + q] = jnp.dot(gt[sm[11, p]], xs, preferred_element_type=F32).astype(cast)
            return 0

        lax.fori_loop(0, 8, one, 0, unroll=True)

    def tiles8(ref, yy):
        return ref.at[pl.ds(yy * 8, 8)]

    dc = {}
    for k in (1, 2, 3, 0):
        yy = lax.rem(y + k, 4)
        tile_grad(1 - d, yy, dt, BF16)
        dc[k] = net.send(tiles8(dt, yy), tiles8(dr, yy), core)
    reduce_other(2)
    reduce_other(3)
    ty = {}
    for k in (1, 2, 3, 0):
        yy = lax.rem(y + k, 4)
        tile_grad(d, yy, e, F32)
        net.recv(dc[k], tiles8(dr, yy))

        def join(q, _):
            i = yy * 8 + q
            v = e[i] + dr[i].astype(F32)
            if k:
                es[i] = v.astype(BF16)
            else:
                e[i] = v
            return 0

        lax.fori_loop(0, 8, join, 0)
        if k:
            ty[k] = net.send(tiles8(es, yy), yr.at[k - 1], y_peer(k))

    def gain_part(rt, _):
        v = s[:, rt].astype(F32) * x_all[:, rt].astype(F32)
        gp[rt] = jnp.sum(v.reshape(256, 128), axis=0, keepdims=True)
        return 0

    lax.fori_loop(0, RT, gain_part, 0)
    gid = net.send(gp.at[pl.ds((1 - d) * 16, 16)], gc, core)

    def ahead(b, acc):
        for u in range(4):
            i = b * 4 + u
            xs = x_all[:, sm[6, i]].reshape(256, 128)
            prod = jnp.dot(xs, w[sm[5, i]], preferred_element_type=F32)
            acc = acc * sm[7, i].astype(F32) + prod
            pf[i] = acc.astype(BF16)
        return acc

    lax.fori_loop(0, SLOTS // 4, ahead, jnp.zeros((256, 128), F32))
    for c in range(CT):
        v = pf[sm[8, c]].astype(F32) * sm[9, c].astype(F32)
        mx[:, c * 128 : (c + 1) * 128] = v.astype(BF16)
    mixed_out = pltpu.make_async_copy(mx, mixed_hbm, lsem.at[5])
    mixed_out.start()

    net.recv(gid, gc)
    for i in range(16):
        g1[i] = gp[d * 16 + i] + gc[i]
    gids = [net.send(g1.at[pl.ds(lax.rem(x + k, 4) * 4, 4)], gx4.at[k - 1], x_peer(k)) for k in (1, 2, 3)]

    for k in (1, 2, 3):
        for q in range(4):
            net.recv(rs_own[q][k - 1], r.at[1, k - 1, pl.ds(q * 8, 8)])

    def own(rt, _):
        v = s[t, rt].astype(F32) + r[1, 0, rt].astype(F32)
        ig[rt] = v + r[1, 1, rt].astype(F32) + r[1, 2, rt].astype(F32)
        return 0

    lax.fori_loop(0, RT, own, 0)

    for k in (1, 2, 3):
        net.recv(gids[k - 1], gx4.at[k - 1])
    for i in range(4):
        gy[y, i] = g1[x * 4 + i] + gx4[0, i] + gx4[1, i] + gx4[2, i]
    gids = [net.send(gy.at[y], gy.at[y], y_peer(k)) for k in (1, 2, 3)]

    for k in (1, 2, 3):
        net.recv(ty[k], yr.at[k - 1])

    def sum_y(q):
        v = e[y * 8 + q] + yr[0, q].astype(F32)
        return v + yr[1, q].astype(F32) + yr[2, q].astype(F32)

    for q in range(4, 8):
        fs[q] = sum_y(q).astype(BF16)
    tz1 = net.send(fs.at[pl.ds(4, 4)], fr.at[pl.ds(4, 4)], z1)
    for q in range(4):
        fa[q] = sum_y(q)

    for k in (1, 2, 3):
        net.recv(gids[k - 1], gy.at[lax.rem(y + 4 - k, 4)])
    for i in range(4):
        gh[0, i] = gy[0, i] + gy[1, i] + gy[2, i] + gy[3, i]
    gid = net.send(gh.at[0], gh.at[1], other_half)

    net.recv(tz1, fr.at[pl.ds(4, 4)])
    for q in (2, 3):
        fs[q] = (fa[q] + fr[q + 4].astype(F32)).astype(BF16)
    tz2 = net.send(fs.at[pl.ds(2, 2)], fr.at[pl.ds(2, 2)], z2)
    for q in (0, 1):
        fa[q] = fa[q] + fr[q + 4].astype(F32)

    net.recv(gid, gh.at[1])
    for i in range(4):
        gz[0, i] = gh[0, i] + gh[1, i]
    gid = net.send(gz.at[0], gz.at[1], z4)

    net.recv(tz2, fr.at[pl.ds(2, 2)])
    fs[1] = (fa[1] + fr[3].astype(F32)).astype(BF16)
    tz3 = net.send(fs.at[pl.ds(1, 1)], fr.at[pl.ds(1, 1)], z4)
    fa[0] = fa[0] + fr[2].astype(F32)

    net.recv(gid, gz.at[1])
    for i in range(4):
        gz[2, i] = gz[0, i] + gz[1, i]
    gid = net.send(gz.at[2], gz.at[3], z2)

    def hidden(rt, a):
        v = (ig[rt] + zr[rt].astype(F32)) * gain[pl.ds(rt, 1), :]
        ig[rt] = v
        return a + v * scaled[rt]

    acc = jnp.zeros((32, 128), F32)
    for q in range(2):
        net.recv(zids[q], zr.at[pl.ds(q * 8, 8)])
        acc = lax.fori_loop(q * 8, q * 8 + 8, hidden, acc)

    net.recv(gid, gz.at[3])
    for i in range(4):
        gz[4, i] = gz[2, i] + gz[3, i]
    gid = net.send(gz.at[4], gz.at[5], z1)

    net.recv(tz3, fr.at[pl.ds(1, 1)])
    keep = jnp.where(counts_s[0, f] > d, 1.0, 0.0)
    tiles[d] = (fa[0] + fr[1].astype(F32)).T * keep
    tc = net.send(tiles.at[d], tiles.at[d], core)

    for q in range(2, 4):
        net.recv(zids[q], zr.at[pl.ds(q * 8, 8)])
        acc = lax.fori_loop(q * 8, q * 8 + 8, hidden, acc)

    net.recv(gid, gz.at[5])
    mine = d * 16 + x * 4
    for i in range(4):
        ga[mine + i] = (gz[4, i] + gz[5, i]) / gain[pl.ds(mine + i, 1), :]
    gids = [net.send(ga.at[pl.ds(mine, 4)], ga.at[pl.ds(mine, 4)], x_peer(k)) for k in (1, 2, 3)]

    mean = jnp.sum(acc, axis=1, keepdims=True) * (1.0 / 4096.0)

    def finish(i, _):
        for u in range(4):
            rt = i * 4 + u
            v = inv[...] * (ig[rt] - scaled[rt] * mean)
            ox[:, lanes(rt)] = v.astype(BF16)
        return 0

    lax.fori_loop(0, RT // 4, finish, 0)
    gx_out = pltpu.make_async_copy(ox, gx_hbm, lsem.at[6])
    gx_out.start()

    for k in (1, 2, 3):
        net.recv(gids[k - 1], ga.at[pl.ds(d * 16 + lax.rem(x + 4 - k, 4) * 4, 4)])
    gid = net.send(ga.at[pl.ds(d * 16, 16)], ga.at[pl.ds(d * 16, 16)], core)
    net.recv(tc, tiles.at[1 - d])
    gt_out = pltpu.make_async_copy(tiles, gt_hbm, lsem.at[7])
    gt_out.start()
    net.recv(gid, ga.at[pl.ds((1 - d) * 16, 16)])
    gg_out = pltpu.make_async_copy(ga, gg_hbm, lsem.at[8])
    gg_out.start()
    for copy in net.sent:
        copy.wait_send()
    for copy in (mixed_out, gx_out, gt_out, gg_out):
        copy.wait()


def per_device(tokens, norm_gain, tile_values, tile_rows, tile_cols, tile_counts, grad_out):
    hbm = pl.BlockSpec(memory_space=pl.ANY)
    vmem = pl.BlockSpec(memory_space=pltpu.VMEM)
    smem = pl.BlockSpec(memory_space=pltpu.SMEM)
    rows8 = (8, RT, 32, 128)
    local = (RT, 32, 128)
    tiles32 = (32, 128, 128)
    mixed, grad_x, grad_gain, grad_tiles = pl.pallas_call(
        kernel,
        out_shape=(
            jax.ShapeDtypeStruct((256, 1792), BF16),
            jax.ShapeDtypeStruct((32, 4096), BF16),
            jax.ShapeDtypeStruct((RT, 1, 128), F32),
            jax.ShapeDtypeStruct((2, 128, 128), F32),
        ),
        in_specs=[hbm, vmem, hbm, vmem, vmem, vmem, smem, hbm],
        out_specs=(hbm, hbm, hbm, hbm),
        scratch_shapes=[
            pltpu.VMEM((32, 4096), BF16),
            pltpu.VMEM((256, 1792), BF16),
            pltpu.VMEM((CT, 256, 128), BF16),
            pltpu.VMEM((CT, 128, 256), BF16),
            pltpu.VMEM(rows8, BF16),
            pltpu.VMEM(local, F32),
            pltpu.VMEM((32, 128), F32),
            pltpu.VMEM((SLOTS, 128, 128), BF16),
            pltpu.VMEM((SLOTS, 256, 128), BF16),
            pltpu.VMEM((SLOTS, 256, 128), BF16),
            pltpu.VMEM(rows8, BF16),
            pltpu.VMEM((2, 3) + local, BF16),
            pltpu.VMEM(local, BF16),
            pltpu.VMEM(local, BF16),
            pltpu.VMEM(local, F32),
            pltpu.VMEM(tiles32, BF16),
            pltpu.VMEM(tiles32, BF16),
            pltpu.VMEM(tiles32, F32),
            pltpu.VMEM(tiles32, BF16),
            pltpu.VMEM((3, 8, 128, 128), BF16),
            pltpu.VMEM((8, 128, 128), BF16),
            pltpu.VMEM((4, 128, 128), F32),
            pltpu.VMEM((8, 128, 128), BF16),
            pltpu.VMEM((2, 128, 128), F32),
            pltpu.VMEM((256, 1792), BF16),
            pltpu.VMEM((32, 4096), BF16),
            pltpu.VMEM((16, 128), jnp.int32),
            pltpu.SMEM((16, 128), jnp.int32),
            pltpu.VMEM((RT, 1, 128), F32),
            pltpu.VMEM((16, 1, 128), F32),
            pltpu.VMEM((16, 1, 128), F32),
            pltpu.VMEM((3, 4, 1, 128), F32),
            pltpu.VMEM((4, 4, 1, 128), F32),
            pltpu.VMEM((2, 4, 1, 128), F32),
            pltpu.VMEM((6, 4, 1, 128), F32),
            pltpu.VMEM((RT, 1, 128), F32),
            pltpu.SemaphoreType.DMA((NSEM,)),
            pltpu.SemaphoreType.DMA((NSEM,)),
            pltpu.SemaphoreType.DMA((9,)),
        ],
        compiler_params=pltpu.CompilerParams(
            collective_id=0, has_side_effects=True, vmem_limit_bytes=52 * 1024 * 1024
        ),
        name="sparse_mlp",
    )(
        tokens, norm_gain.reshape(RT, 128), tile_values, tile_rows, tile_cols, tile_counts,
        tile_counts, grad_out,
    )
    return mixed, grad_x, grad_gain.reshape(4096), grad_tiles


def solution(mesh):
    placed = (
        P(("dp", "fsdp", "tensor"), None),
        P(),
        P(("fsdp", "tensor"), None, None),
        P("tensor", None),
        P("tensor", None),
        P("tensor", None),
        P(("dp", "fsdp"), "tensor"),
    )
    return jax.shard_map(
        per_device,
        mesh=mesh,
        in_specs=placed,
        out_specs=(
            P(("dp", "fsdp"), "tensor"),
            P(("dp", "fsdp", "tensor"), None),
            P(),
            P(("fsdp", "tensor"), None, None),
        ),
        check_vma=False,
    )
```

```python
import functools

import jax
import jax.numpy as jnp
from jax import lax
from jax.experimental import pallas as pl
from jax.experimental.pallas import tpu as pltpu
from jax.sharding import PartitionSpec as P

MESH = pl.DeviceIdType.MESH
F32 = jnp.float32
BF16 = jnp.bfloat16
RT = 32
CT = 14
SLOTS = 64
NSEM = 160
X_OVER = (0, 2, 3, 3)


class Net:
    def __init__(self, ssem, rsem, anyone):
        self.ssem, self.rsem, self.anyone = ssem, rsem, anyone
        self.sent = []

    def send(self, src, dst, device):
        i = len(self.sent)
        copy = pltpu.make_async_remote_copy(
            src_ref=src,
            dst_ref=dst,
            send_sem=self.ssem.at[i],
            recv_sem=self.rsem.at[i],
            device_id=device,
            device_id_type=MESH,
        )
        copy.start()
        self.sent.append(copy)
        return i

    def recv(self, i, ref):
        pltpu.make_async_remote_copy(
            src_ref=ref,
            dst_ref=ref,
            send_sem=self.ssem.at[i],
            recv_sem=self.rsem.at[i],
            device_id=self.anyone,
            device_id_type=MESH,
        ).wait_recv()


def lanes(i):
    return pl.ds(pl.multiple_of(i * 128, 128), 128)


def slot_tables(rows, cols, counts, zl, table):
    sub = lax.broadcasted_iota(jnp.int32, (SLOTS, SLOTS), 0)
    lane = lax.broadcasted_iota(jnp.int32, (SLOTS, SLOTS), 1)
    wide = lax.broadcasted_iota(jnp.int32, (SLOTS, 128), 1)
    slot = lax.broadcasted_iota(jnp.int32, (SLOTS, 1), 0)

    def over_lanes(mask, value):
        return jnp.sum(jnp.where(mask, value, 0), axis=1, keepdims=True)

    def over_slots(mask, value):
        return jnp.sum(jnp.where(mask, value, 0), axis=0, keepdims=True)

    def row(column_vector):
        return over_slots(sub == lane, column_vector)

    def put(k, vector):
        table[pl.ds(k, 1), :] = vector

    table[...] = jnp.zeros_like(table)
    row_of, col_of = over_lanes(sub == lane, rows), over_lanes(sub == lane, cols)
    shard = lax.broadcasted_iota(jnp.int32, (SLOTS, 32), 0) >> 1
    shard_lane = lax.broadcasted_iota(jnp.int32, (SLOTS, 32), 1)
    count = over_lanes(shard == shard_lane, counts)
    j = slot & 1
    held = count > j
    apart = ((slot >> 1) & 7) ^ zl
    place = ((apart & 1) << 2) | (apart & 2) | (apart >> 2)
    stored = j * 32 + (slot >> 4) * 8 + place
    for base, key, other in ((0, row_of, col_of), (5, col_of, row_of)):
        key = jnp.where(held, key, 64)
        order = key * 64 + slot
        rank = over_lanes(row(order) < order, 1)
        same = over_lanes((row(key) == key) & (lane < sub), 1)
        at = rank == wide
        for k, vector in ((0, stored), (1, other), (2, jnp.minimum(same, 1))):
            put(base + k, over_slots(at, vector))
        put(base + 3, jnp.maximum(over_slots(key <= wide, 1) - 1, 0))
        put(base + 4, jnp.minimum(over_slots(key == wide, 1), 1))
    at = stored == wide
    put(10, over_slots(at, row_of))
    put(11, over_slots(at, col_of))


def kernel(
    tok_hbm, gain, tv_hbm, rows, cols, counts, counts_s, go_hbm,
    mixed_hbm, gx_hbm, gg_hbm, gt_hbm,
    tok, go, gs, gt, x_all, scaled, inv, w, pb, pf, s, r, zs, zr, ig,
    dt, dr, e, es, yr, fs, fa, fr, tiles, mx, ox, table, sm,
    gp, gc, gy, gz, ga, ssem, rsem, lsem,
):
    d, f, t = lax.axis_index("dp"), lax.axis_index("fsdp"), lax.axis_index("tensor")
    h, x, y, zl = t // 4, lax.rem(t, 4), f // 8, lax.rem(f, 8)
    z = h * 8 + zl
    core = {"dp": 1 - d}
    oc = lax.rem(t + 4, 8)
    other_half = {"tensor": oc}

    def x_peer(k, dd=0):
        peer = {"tensor": h * 4 + lax.rem(x + k, 4)}
        return {**peer, "dp": 1 - d} if dd else peer

    def y_peer(k):
        return {"fsdp": lax.rem(y + k, 4) * 8 + zl}

    def z_peer(k):
        to = lax.rem(z + k, 16)
        return {"fsdp": y * 8 + lax.rem(to, 8), "tensor": (to // 8) * 4 + x}

    z4 = {"fsdp": y * 8 + lax.rem(zl + 4, 8)}
    z2 = {"fsdp": f + 2 - 4 * lax.rem(zl // 2, 2)}
    z1 = {"fsdp": f + 1 - 2 * lax.rem(zl, 2)}
    plane = [(dd, k) for dd in (0, 1) for k in range(4) if dd or k]
    partners = [x_peer(k, dd) for dd, k in plane]
    partners += [y_peer(k) for k in (1, 2, 3)] + [z_peer(k) for k in range(1, 16)]

    own_w = d * 32 + y * 8
    other_w = (1 - d) * 32

    loads = [
        pltpu.make_async_copy(tok_hbm, tok, lsem.at[0]),
        pltpu.make_async_copy(tv_hbm.at[0], w.at[y * 8], lsem.at[1]),
        pltpu.make_async_copy(tv_hbm.at[1], w.at[32 + y * 8], lsem.at[2]),
        pltpu.make_async_copy(go_hbm, go, lsem.at[3]),
    ]
    for c in loads:
        c.start()
    barrier = pltpu.get_barrier_semaphore()
    for p in partners:
        pl.semaphore_signal(barrier, inc=1, device_id=p, device_id_type=MESH)

    def square(i, a):
        for u in range(4):
            v = tok[:, lanes(i * 4 + u)].astype(F32)
            a = a + v * v
        return a

    def norm(i, _):
        for u in range(4):
            rt = i * 4 + u
            v = tok[:, lanes(rt)].astype(F32) * inv[...]
            scaled[rt] = v
            x_all[t, rt] = (v * gain[pl.ds(rt, 1), :]).astype(BF16)
        return 0

    loads[0].wait()
    total = lax.fori_loop(0, RT // 4, square, jnp.zeros((32, 128), F32))
    inv_rms = lax.rsqrt(jnp.sum(total, axis=1, keepdims=True) * (1.0 / 4096.0) + 1e-05)
    inv[...] = jnp.broadcast_to(inv_rms, (32, 128))
    loads[1].wait()
    loads[2].wait()
    pl.semaphore_wait(barrier, len(partners))

    net = Net(ssem, rsem, core)

    def w_at(base, lo, n):
        return w.at[pl.ds(base + lo, n)]

    def w_to_y(lo, n):
        return [net.send(w_at(own_w, lo, n), w_at(own_w, lo, n), y_peer(k)) for k in (1, 2, 3)]

    def x_chunk(c, q):
        return x_all.at[c, pl.ds(q * 8, 8)]

    xz, xfwd = [], []

    def x_over(q):
        xz.append(net.send(x_chunk(t, q), x_chunk(t, q), other_half))

    def forward(q):
        net.recv(xz[q], x_chunk(oc, q))
        xfwd.append([net.send(x_chunk(oc, q), x_chunk(oc, q), x_peer(k)) for k in (1, 2, 3)])

    wz = [net.send(w_at(own_w, 0, 1), w_at(own_w, 1, 1), z4)]
    wy = [w_to_y(0, 1)]
    lax.fori_loop(0, RT // 4, norm, 0)
    if X_OVER[0] == 0:
        x_over(0)
    xown = [net.send(x_all.at[t], x_all.at[t], x_peer(k)) for k in (1, 2, 3)]

    net.recv(wz[0], w_at(own_w, 1, 1))
    wz.append(net.send(w_at(own_w, 0, 2), w_at(own_w, 2, 2), z2))
    wy.append(w_to_y(1, 1))
    for q in range(4):
        if X_OVER[q] == 1:
            x_over(q)
    slot_tables(rows[...], cols[...], counts[...], zl, table)
    to_smem = pltpu.make_async_copy(table, sm, lsem.at[4])
    to_smem.start()

    net.recv(wz[1], w_at(own_w, 2, 2))
    wz.append(net.send(w_at(own_w, 0, 4), w_at(own_w, 4, 4), z1))
    wy.append(w_to_y(2, 2))
    for q in range(4):
        if X_OVER[q] == 2:
            x_over(q)
    loads[3].wait()
    for c in range(CT):
        v = go[:, c * 128 : (c + 1) * 128]
        gs[c] = v
        gt[c] = v.T

    net.recv(wz[2], w_at(own_w, 4, 4))
    wy.append(w_to_y(4, 4))
    wc = [net.send(w_at(own_w, 1, 7), w_at(own_w, 1, 7), core)]
    for q in range(4):
        if X_OVER[q] == 3:
            x_over(q)
    forward(0)
    for k in (1, 2, 3):
        base = d * 32 + lax.rem(y + 4 - k, 4) * 8
        for ids, (lo, n) in zip(wy, ((0, 1), (1, 1), (2, 2), (4, 4))):
            net.recv(ids[k - 1], w_at(base, lo, n))
        wc.append(net.send(w_at(base, 0, 8), w_at(base, 0, 8), core))
    net.recv(wc[0], w_at(other_w + y * 8, 1, 7))
    for k in (1, 2, 3):
        net.recv(wc[k], w_at(other_w + lax.rem(y + 4 - k, 4) * 8, 0, 8))
    to_smem.wait()

    def back(b, acc):
        for u in range(4):
            i = b * 4 + u
            prod = lax.dot_general(gs[sm[1, i]], w[sm[0, i]], (((1,), (1,)), ((), ())), preferred_element_type=F32)
            acc = acc * sm[2, i].astype(F32) + prod
            pb[i] = acc.astype(BF16)
        return acc

    lax.fori_loop(0, SLOTS // 4, back, jnp.zeros((256, 128), F32))
    rs_other, rs_own = [], []

    def assemble(q):
        def one(rt, _):
            v = pb[sm[3, rt]].astype(F32) * sm[4, rt].astype(F32)
            s[:, rt] = v.astype(BF16).reshape(8, 32, 128)
            return 0

        lax.fori_loop(q * 8, q * 8 + 8, one, 0)

    def scatter(half, slot, q):
        ids = []
        for k in (1, 2, 3):
            to = half * 4 + lax.rem(x + k, 4)
            ids.append(net.send(s.at[to, pl.ds(q * 8, 8)], r.at[slot, k - 1, pl.ds(q * 8, 8)], x_peer(k)))
        return ids

    for q in range(4):
        assemble(q)
        rs_other.append(scatter(1 - h, 0, q))

    zids = []

    def reduce_other(q):
        for k in (1, 2, 3):
            net.recv(rs_other[q][k - 1], r.at[0, k - 1, pl.ds(q * 8, 8)])

        def one(rt, _):
            v = s[oc, rt].astype(F32) + r[0, 0, rt].astype(F32)
            v = v + r[0, 1, rt].astype(F32) + r[0, 2, rt].astype(F32)
            zs[rt] = v.astype(BF16)
            return 0

        lax.fori_loop(q * 8, q * 8 + 8, one, 0)
        part = pl.ds(q * 8, 8)
        zids.append(net.send(zs.at[part], zr.at[part], other_half))

    forward(1)
    forward(2)
    reduce_other(0)
    forward(3)
    reduce_other(1)
    reduce_other(2)
    reduce_other(3)
    for q in range(4):
        rs_own.append(scatter(h, 1, q))
    for k in (1, 2, 3):
        net.recv(xown[k - 1], x_all.at[h * 4 + lax.rem(x + 4 - k, 4)])
        for q in range(4):
            net.recv(xfwd[q][k - 1], x_chunk((1 - h) * 4 + lax.rem(x + 4 - k, 4), q))

    def tile_grad(first, out, at, cast):
        def one(q, _):
            p = first + q
            xs = x_all[:, sm[10, p]].reshape(256, 128)
            out[at + q] = jnp.dot(gt[sm[11, p]], xs, preferred_element_type=F32).astype(cast)
            return 0

        lax.fori_loop(0, 4, one, 0, unroll=True)

    def tiles4(ref, at):
        return ref.at[pl.ds(at, 4)]

    order = [(lo, k) for lo in (4, 0) for k in (1, 2, 3, 0)]
    dc, ty = {}, {}
    for lo, k in order:
        at = lax.rem(y + k, 4) * 8 + lo
        tile_grad(other_w + at, dt, at, BF16)
        dc[lo, k] = net.send(tiles4(dt, at), tiles4(dr, at), core)
    for lo, k in order:
        at = lax.rem(y + k, 4) * 8 + lo
        tile_grad(d * 32 + at, e, at, F32)
        net.recv(dc[lo, k], tiles4(dr, at))

        def join(q, _):
            v = e[at + q] + dr[at + q].astype(F32)
            if k:
                es[at + q] = v.astype(BF16)
            else:
                e[at + q] = v
            return 0

        lax.fori_loop(0, 4, join, 0)
        if k:
            ty[lo, k] = net.send(tiles4(es, at), yr.at[k - 1, pl.ds(lo, 4)], y_peer(k))

    def gain_part(rt, _):
        v = s[:, rt].astype(F32) * x_all[:, rt].astype(F32)
        gp[rt] = jnp.sum(v.reshape(256, 128), axis=0, keepdims=True)
        return 0

    lax.fori_loop(0, RT, gain_part, 0)

    def piece(dd, k):
        return lax.rem(d + dd, 2) * 16 + lax.rem(x + k, 4) * 4

    gids = [net.send(gp.at[pl.ds(piece(dd, k), 4)], gc.at[i], x_peer(k, dd)) for i, (dd, k) in enumerate(plane)]

    def ahead(b, acc):
        for u in range(4):
            i = b * 4 + u
            xs = x_all[:, sm[6, i]].reshape(256, 128)
            prod = jnp.dot(xs, w[sm[5, i]], preferred_element_type=F32)
            acc = acc * sm[7, i].astype(F32) + prod
            pf[i] = acc.astype(BF16)
        return acc

    acc = lax.fori_loop(0, SLOTS // 8, ahead, jnp.zeros((256, 128), F32))
    mine = d * 16 + x * 4
    for i in range(7):
        net.recv(gids[i], gc.at[i])
    for i in range(4):
        v = gp[mine + i]
        for k in range(7):
            v = v + gc[k, i]
        gy[y, i] = v
    gids = [net.send(gy.at[y], gy.at[y], y_peer(k)) for k in (1, 2, 3)]

    lax.fori_loop(SLOTS // 8, SLOTS // 4, ahead, acc)
    for c in range(CT):
        v = pf[sm[8, c]].astype(F32) * sm[9, c].astype(F32)
        mx[:, c * 128 : (c + 1) * 128] = v.astype(BF16)
    mixed_out = pltpu.make_async_copy(mx, mixed_hbm, lsem.at[5])
    mixed_out.start()

    for k in (1, 2, 3):
        net.recv(gids[k - 1], gy.at[lax.rem(y + 4 - k, 4)])
    for i in range(4):
        gz[z, i] = gy[0, i] + gy[1, i] + gy[2, i] + gy[3, i]
    gids = [net.send(gz.at[z], gz.at[z], z_peer(k)) for k in range(1, 16)]

    def sum_y(q):
        v = e[y * 8 + q] + yr[0, q].astype(F32)
        return v + yr[1, q].astype(F32) + yr[2, q].astype(F32)

    for k in (1, 2, 3):
        net.recv(ty[4, k], yr.at[k - 1, pl.ds(4, 4)])
    for q in range(4, 8):
        fs[q] = sum_y(q).astype(BF16)
    tz1 = net.send(fs.at[pl.ds(4, 4)], fr.at[pl.ds(4, 4)], z1)
    for k in (1, 2, 3):
        net.recv(ty[0, k], yr.at[k - 1, pl.ds(0, 4)])
    for q in range(4):
        fa[q] = sum_y(q)

    net.recv(tz1, fr.at[pl.ds(4, 4)])
    for q in (2, 3):
        fs[q] = (fa[q] + fr[q + 4].astype(F32)).astype(BF16)
    tz2 = net.send(fs.at[pl.ds(2, 2)], fr.at[pl.ds(2, 2)], z2)
    for q in (0, 1):
        fa[q] = fa[q] + fr[q + 4].astype(F32)

    for k in (1, 2, 3):
        for q in range(4):
            net.recv(rs_own[q][k - 1], r.at[1, k - 1, pl.ds(q * 8, 8)])

    def own(rt, _):
        v = s[t, rt].astype(F32) + r[1, 0, rt].astype(F32)
        ig[rt] = v + r[1, 1, rt].astype(F32) + r[1, 2, rt].astype(F32)
        return 0

    lax.fori_loop(0, RT, own, 0)

    net.recv(tz2, fr.at[pl.ds(2, 2)])
    fs[1] = (fa[1] + fr[3].astype(F32)).astype(BF16)
    tz3 = net.send(fs.at[pl.ds(1, 1)], fr.at[pl.ds(1, 1)], z4)
    fa[0] = fa[0] + fr[2].astype(F32)

    for k in range(1, 16):
        net.recv(gids[k - 1], gz.at[lax.rem(z + 16 - k, 16)])
    for i in range(4):
        v = gz[0, i]
        for k in range(1, 16):
            v = v + gz[k, i]
        ga[mine + i] = v / gain[pl.ds(mine + i, 1), :]
    gids = [net.send(ga.at[pl.ds(mine, 4)], ga.at[pl.ds(mine, 4)], x_peer(k, dd)) for dd, k in plane]

    def hidden(rt, a):
        v = (ig[rt] + zr[rt].astype(F32)) * gain[pl.ds(rt, 1), :]
        ig[rt] = v
        return a + v * scaled[rt]

    acc = jnp.zeros((32, 128), F32)
    for q in range(4):
        net.recv(zids[q], zr.at[pl.ds(q * 8, 8)])
        acc = lax.fori_loop(q * 8, q * 8 + 8, hidden, acc)
    mean = jnp.sum(acc, axis=1, keepdims=True) * (1.0 / 4096.0)

    def finish(i, _):
        for u in range(4):
            rt = i * 4 + u
            v = inv[...] * (ig[rt] - scaled[rt] * mean)
            ox[:, lanes(rt)] = v.astype(BF16)
        return 0

    lax.fori_loop(0, RT // 4, finish, 0)
    gx_out = pltpu.make_async_copy(ox, gx_hbm, lsem.at[6])
    gx_out.start()

    net.recv(tz3, fr.at[pl.ds(1, 1)])
    keep = jnp.where(counts_s[0, f] > d, 1.0, 0.0)
    tiles[d] = (fa[0] + fr[1].astype(F32)).T * keep
    tc = net.send(tiles.at[d], tiles.at[d], core)

    for i, (dd, k) in enumerate(plane):
        net.recv(gids[i], ga.at[pl.ds(piece(dd, 4 - k), 4)])
    gg_out = pltpu.make_async_copy(ga, gg_hbm, lsem.at[8])
    gg_out.start()
    net.recv(tc, tiles.at[1 - d])
    gt_out = pltpu.make_async_copy(tiles, gt_hbm, lsem.at[7])
    gt_out.start()
    for copy in net.sent:
        copy.wait_send()
    for copy in (mixed_out, gx_out, gt_out, gg_out):
        copy.wait()


def per_device(tokens, norm_gain, tile_values, tile_rows, tile_cols, tile_counts, grad_out):
    hbm = pl.BlockSpec(memory_space=pl.ANY)
    vmem = pl.BlockSpec(memory_space=pltpu.VMEM)
    smem = pl.BlockSpec(memory_space=pltpu.SMEM)
    rows8 = (8, RT, 32, 128)
    local = (RT, 32, 128)
    tiles32 = (32, 128, 128)
    mixed, grad_x, grad_gain, grad_tiles = pl.pallas_call(
        kernel,
        out_shape=(
            jax.ShapeDtypeStruct((256, 1792), BF16),
            jax.ShapeDtypeStruct((32, 4096), BF16),
            jax.ShapeDtypeStruct((RT, 1, 128), F32),
            jax.ShapeDtypeStruct((2, 128, 128), F32),
        ),
        in_specs=[hbm, vmem, hbm, vmem, vmem, vmem, smem, hbm],
        out_specs=(hbm, hbm, hbm, hbm),
        scratch_shapes=[
            pltpu.VMEM((32, 4096), BF16),
            pltpu.VMEM((256, 1792), BF16),
            pltpu.VMEM((CT, 256, 128), BF16),
            pltpu.VMEM((CT, 128, 256), BF16),
            pltpu.VMEM(rows8, BF16),
            pltpu.VMEM(local, F32),
            pltpu.VMEM((32, 128), F32),
            pltpu.VMEM((SLOTS, 128, 128), BF16),
            pltpu.VMEM((SLOTS, 256, 128), BF16),
            pltpu.VMEM((SLOTS, 256, 128), BF16),
            pltpu.VMEM(rows8, BF16),
            pltpu.VMEM((2, 3) + local, BF16),
            pltpu.VMEM(local, BF16),
            pltpu.VMEM(local, BF16),
            pltpu.VMEM(local, F32),
            pltpu.VMEM(tiles32, BF16),
            pltpu.VMEM(tiles32, BF16),
            pltpu.VMEM(tiles32, F32),
            pltpu.VMEM(tiles32, BF16),
            pltpu.VMEM((3, 8, 128, 128), BF16),
            pltpu.VMEM((8, 128, 128), BF16),
            pltpu.VMEM((4, 128, 128), F32),
            pltpu.VMEM((8, 128, 128), BF16),
            pltpu.VMEM((2, 128, 128), F32),
            pltpu.VMEM((256, 1792), BF16),
            pltpu.VMEM((32, 4096), BF16),
            pltpu.VMEM((16, 128), jnp.int32),
            pltpu.SMEM((16, 128), jnp.int32),
            pltpu.VMEM((RT, 1, 128), F32),
            pltpu.VMEM((7, 4, 1, 128), F32),
            pltpu.VMEM((4, 4, 1, 128), F32),
            pltpu.VMEM((16, 4, 1, 128), F32),
            pltpu.VMEM((RT, 1, 128), F32),
            pltpu.SemaphoreType.DMA((NSEM,)),
            pltpu.SemaphoreType.DMA((NSEM,)),
            pltpu.SemaphoreType.DMA((9,)),
        ],
        compiler_params=pltpu.CompilerParams(
            collective_id=0, has_side_effects=True, vmem_limit_bytes=62 * 1024 * 1024
        ),
        name="sparse_mlp",
    )(
        tokens, norm_gain.reshape(RT, 128), tile_values, tile_rows, tile_cols, tile_counts,
        tile_counts, grad_out,
    )
    return mixed, grad_x, grad_gain.reshape(4096), grad_tiles


def solution(mesh):
    placed = (
        P(("dp", "fsdp", "tensor"), None),
        P(),
        P(("fsdp", "tensor"), None, None),
        P("tensor", None),
        P("tensor", None),
        P("tensor", None),
        P(("dp", "fsdp"), "tensor"),
    )
    return jax.shard_map(
        per_device,
        mesh=mesh,
        in_specs=placed,
        out_specs=(
            P(("dp", "fsdp"), "tensor"),
            P(("dp", "fsdp", "tensor"), None),
            P(),
            P(("fsdp", "tensor"), None, None),
        ),
        check_vma=False,
    )
```

```python
import functools

import jax
import jax.numpy as jnp
from jax import lax
from jax.experimental import pallas as pl
from jax.experimental.pallas import tpu as pltpu
from jax.sharding import PartitionSpec as P

MESH = pl.DeviceIdType.MESH
F32 = jnp.float32
BF16 = jnp.bfloat16
RT = 32
CT = 14
SLOTS = 64
NSEM = 160
X_OVER = (1, 2, 3, 3)
FORWARD = (0, 1, 2, 3)
TILES_AT = 2


class Net:
    def __init__(self, ssem, rsem, anyone):
        self.ssem, self.rsem, self.anyone = ssem, rsem, anyone
        self.sent = []

    def send(self, src, dst, device):
        i = len(self.sent)
        copy = pltpu.make_async_remote_copy(
            src_ref=src,
            dst_ref=dst,
            send_sem=self.ssem.at[i],
            recv_sem=self.rsem.at[i],
            device_id=device,
            device_id_type=MESH,
        )
        copy.start()
        self.sent.append(copy)
        return i

    def recv(self, i, ref):
        pltpu.make_async_remote_copy(
            src_ref=ref,
            dst_ref=ref,
            send_sem=self.ssem.at[i],
            recv_sem=self.rsem.at[i],
            device_id=self.anyone,
            device_id_type=MESH,
        ).wait_recv()


def lanes(i):
    return pl.ds(pl.multiple_of(i * 128, 128), 128)


def slot_tables(rows, cols, counts, zl, table):
    sub = lax.broadcasted_iota(jnp.int32, (SLOTS, SLOTS), 0)
    lane = lax.broadcasted_iota(jnp.int32, (SLOTS, SLOTS), 1)
    wide = lax.broadcasted_iota(jnp.int32, (SLOTS, 128), 1)
    slot = lax.broadcasted_iota(jnp.int32, (SLOTS, 1), 0)

    def over_lanes(mask, value):
        return jnp.sum(jnp.where(mask, value, 0), axis=1, keepdims=True)

    def over_slots(mask, value):
        return jnp.sum(jnp.where(mask, value, 0), axis=0, keepdims=True)

    def row(column_vector):
        return over_slots(sub == lane, column_vector)

    def put(k, vector):
        table[pl.ds(k, 1), :] = vector

    table[...] = jnp.zeros_like(table)
    row_of, col_of = over_lanes(sub == lane, rows), over_lanes(sub == lane, cols)
    shard = lax.broadcasted_iota(jnp.int32, (SLOTS, 32), 0) >> 1
    shard_lane = lax.broadcasted_iota(jnp.int32, (SLOTS, 32), 1)
    count = over_lanes(shard == shard_lane, counts)
    j = slot & 1
    held = count > j
    apart = ((slot >> 1) & 7) ^ zl
    place = ((apart & 1) << 2) | (apart & 2) | (apart >> 2)
    stored = j * 32 + (slot >> 4) * 8 + place
    for base, key, other in ((0, row_of, col_of), (5, col_of, row_of)):
        key = jnp.where(held, key, 64)
        order = key * 64 + slot
        rank = over_lanes(row(order) < order, 1)
        same = over_lanes((row(key) == key) & (lane < sub), 1)
        at = rank == wide
        for k, vector in ((0, stored), (1, other), (2, jnp.minimum(same, 1))):
            put(base + k, over_slots(at, vector))
        put(base + 3, jnp.maximum(over_slots(key <= wide, 1) - 1, 0))
        put(base + 4, jnp.minimum(over_slots(key == wide, 1), 1))
    at = stored == wide
    put(10, over_slots(at, row_of))
    put(11, over_slots(at, col_of))


def kernel(
    tok_hbm, gain, tv_hbm, rows, cols, counts, counts_s, go_hbm,
    mixed_hbm, gx_hbm, gg_hbm, gt_hbm,
    tok, go, gs, gt, x_all, scaled, inv, w, pb, pf, s, r, zs, zr, ig,
    dt, dr, e, es, yr, fs, fa, fr, tiles, mx, ox, table, sm,
    gp, gc, gy, gz, ga, ssem, rsem, lsem,
):
    d, f, t = lax.axis_index("dp"), lax.axis_index("fsdp"), lax.axis_index("tensor")
    h, x, y, zl = t // 4, lax.rem(t, 4), f // 8, lax.rem(f, 8)
    z = h * 8 + zl
    core = {"dp": 1 - d}
    oc = lax.rem(t + 4, 8)
    other_half = {"tensor": oc}

    def x_peer(k, dd=0):
        peer = {"tensor": h * 4 + lax.rem(x + k, 4)}
        return {**peer, "dp": 1 - d} if dd else peer

    def y_peer(k):
        return {"fsdp": lax.rem(y + k, 4) * 8 + zl}

    def z_peer(k):
        to = lax.rem(z + k, 16)
        return {"fsdp": y * 8 + lax.rem(to, 8), "tensor": (to // 8) * 4 + x}

    z4 = {"fsdp": y * 8 + lax.rem(zl + 4, 8)}
    z2 = {"fsdp": f + 2 - 4 * lax.rem(zl // 2, 2)}
    z1 = {"fsdp": f + 1 - 2 * lax.rem(zl, 2)}
    plane = [(dd, k) for dd in (0, 1) for k in range(4) if dd or k]
    partners = [x_peer(k, dd) for dd, k in plane]
    partners += [y_peer(k) for k in (1, 2, 3)] + [z_peer(k) for k in range(1, 16)]

    own_w = d * 32 + y * 8
    other_w = (1 - d) * 32

    loads = [
        pltpu.make_async_copy(tok_hbm, tok, lsem.at[0]),
        pltpu.make_async_copy(tv_hbm.at[0], w.at[y * 8], lsem.at[1]),
        pltpu.make_async_copy(tv_hbm.at[1], w.at[32 + y * 8], lsem.at[2]),
        pltpu.make_async_copy(go_hbm, go, lsem.at[3]),
    ]
    for c in loads:
        c.start()
    barrier = pltpu.get_barrier_semaphore()
    for p in partners:
        pl.semaphore_signal(barrier, inc=1, device_id=p, device_id_type=MESH)

    def square(i, a):
        for u in range(4):
            v = tok[:, lanes(i * 4 + u)].astype(F32)
            a = a + v * v
        return a

    def norm(i, _):
        for u in range(4):
            rt = i * 4 + u
            v = tok[:, lanes(rt)].astype(F32) * inv[...]
            scaled[rt] = v
            x_all[t, rt] = (v * gain[pl.ds(rt, 1), :]).astype(BF16)
        return 0

    loads[0].wait()
    total = lax.fori_loop(0, RT // 4, square, jnp.zeros((32, 128), F32))
    inv_rms = lax.rsqrt(jnp.sum(total, axis=1, keepdims=True) * (1.0 / 4096.0) + 1e-05)
    inv[...] = jnp.broadcast_to(inv_rms, (32, 128))
    loads[1].wait()
    loads[2].wait()
    pl.semaphore_wait(barrier, len(partners))

    net = Net(ssem, rsem, core)

    def w_at(base, lo, n):
        return w.at[pl.ds(base + lo, n)]

    def w_to_y(lo, n):
        return [net.send(w_at(own_w, lo, n), w_at(own_w, lo, n), y_peer(k)) for k in (1, 2, 3)]

    def x_chunk(c, q):
        return x_all.at[c, pl.ds(q * 8, 8)]

    xz, xfwd = [], []

    def x_over(q):
        xz.append(net.send(x_chunk(t, q), x_chunk(t, q), other_half))

    def forward(q):
        net.recv(xz[q], x_chunk(oc, q))
        xfwd.append([net.send(x_chunk(oc, q), x_chunk(oc, q), x_peer(k)) for k in (1, 2, 3)])

    def forwards(at):
        for q in range(4):
            if FORWARD[q] == at:
                forward(q)

    wz = [net.send(w_at(own_w, 0, 1), w_at(own_w, 1, 1), z4)]
    wy = [w_to_y(0, 1)]
    lax.fori_loop(0, RT // 4, norm, 0)
    for q in range(4):
        if X_OVER[q] == 0:
            x_over(q)
    xown = [net.send(x_all.at[t], x_all.at[t], x_peer(k)) for k in (1, 2, 3)]

    net.recv(wz[0], w_at(own_w, 1, 1))
    wz.append(net.send(w_at(own_w, 0, 2), w_at(own_w, 2, 2), z2))
    wy.append(w_to_y(1, 1))
    for q in range(4):
        if X_OVER[q] == 1:
            x_over(q)

    net.recv(wz[1], w_at(own_w, 2, 2))
    wz.append(net.send(w_at(own_w, 0, 4), w_at(own_w, 4, 4), z1))
    wy.append(w_to_y(2, 2))
    for q in range(4):
        if X_OVER[q] == 2:
            x_over(q)

    net.recv(wz[2], w_at(own_w, 4, 4))
    wy.append(w_to_y(4, 4))
    wc = [net.send(w_at(own_w, 1, 7), w_at(own_w, 1, 7), core)]
    for q in range(4):
        if X_OVER[q] == 3:
            x_over(q)
    slot_tables(rows[...], cols[...], counts[...], zl, table)
    to_smem = pltpu.make_async_copy(table, sm, lsem.at[4])
    to_smem.start()
    loads[3].wait()
    for c in range(CT):
        v = go[:, c * 128 : (c + 1) * 128]
        gs[c] = v
        gt[c] = v.T
    forwards(0)
    for k in (1, 2, 3):
        base = d * 32 + lax.rem(y + 4 - k, 4) * 8
        for ids, (lo, n) in zip(wy, ((0, 1), (1, 1), (2, 2), (4, 4))):
            net.recv(ids[k - 1], w_at(base, lo, n))
        wc.append(net.send(w_at(base, 0, 8), w_at(base, 0, 8), core))
    forwards(1)
    net.recv(wc[0], w_at(other_w + y * 8, 1, 7))
    for k in (1, 2, 3):
        net.recv(wc[k], w_at(other_w + lax.rem(y + 4 - k, 4) * 8, 0, 8))
    to_smem.wait()
    forwards(2)

    def back(b, acc):
        for u in range(4):
            i = b * 4 + u
            prod = lax.dot_general(gs[sm[1, i]], w[sm[0, i]], (((1,), (1,)), ((), ())), preferred_element_type=F32)
            acc = acc * sm[2, i].astype(F32) + prod
            pb[i] = acc.astype(BF16)
        return acc

    lax.fori_loop(0, SLOTS // 4, back, jnp.zeros((256, 128), F32))
    rs_other, rs_own = [], []

    def assemble(q):
        def one(rt, _):
            v = pb[sm[3, rt]].astype(F32) * sm[4, rt].astype(F32)
            s[:, rt] = v.astype(BF16).reshape(8, 32, 128)
            return 0

        lax.fori_loop(q * 8, q * 8 + 8, one, 0)

    def scatter(half, slot, q):
        ids = []
        for k in (1, 2, 3):
            to = half * 4 + lax.rem(x + k, 4)
            ids.append(net.send(s.at[to, pl.ds(q * 8, 8)], r.at[slot, k - 1, pl.ds(q * 8, 8)], x_peer(k)))
        return ids

    for q in range(4):
        assemble(q)
        rs_other.append(scatter(1 - h, 0, q))

    zids = []

    def reduce_other(q):
        for k in (1, 2, 3):
            net.recv(rs_other[q][k - 1], r.at[0, k - 1, pl.ds(q * 8, 8)])

        def one(rt, _):
            v = s[oc, rt].astype(F32) + r[0, 0, rt].astype(F32)
            v = v + r[0, 1, rt].astype(F32) + r[0, 2, rt].astype(F32)
            zs[rt] = v.astype(BF16)
            return 0

        lax.fori_loop(q * 8, q * 8 + 8, one, 0)
        part = pl.ds(q * 8, 8)
        zids.append(net.send(zs.at[part], zr.at[part], other_half))

    def tile_grad(first, out, at, cast):
        def one(q, _):
            p = first + q
            xs = x_all[:, sm[10, p]].reshape(256, 128)
            out[at + q] = jnp.dot(gt[sm[11, p]], xs, preferred_element_type=F32).astype(cast)
            return 0

        lax.fori_loop(0, 4, one, 0, unroll=True)

    def tiles4(ref, at):
        return ref.at[pl.ds(at, 4)]

    order = [(lo, k) for lo in (4, 0) for k in (1, 2, 3, 0)]
    dc, ty = {}, {}

    def tiles_to_core():
        for k in (1, 2, 3):
            net.recv(xown[k - 1], x_all.at[h * 4 + lax.rem(x + 4 - k, 4)])
            for q in range(4):
                net.recv(xfwd[q][k - 1], x_chunk((1 - h) * 4 + lax.rem(x + 4 - k, 4), q))
        for lo, k in order:
            at = lax.rem(y + k, 4) * 8 + lo
            tile_grad(other_w + at, dt, at, BF16)
            dc[lo, k] = net.send(tiles4(dt, at), tiles4(dr, at), core)

    def gain_part(rt, _):
        v = s[:, rt].astype(F32) * x_all[:, rt].astype(F32)
        gp[rt] = jnp.sum(v.reshape(256, 128), axis=0, keepdims=True)
        return 0

    def piece(dd, k):
        return lax.rem(d + dd, 2) * 16 + lax.rem(x + k, 4) * 4

    gids = []

    def gain_to_plane():
        lax.fori_loop(0, RT, gain_part, 0)
        for i, (dd, k) in enumerate(plane):
            gids.append(net.send(gp.at[pl.ds(piece(dd, k), 4)], gc.at[i], x_peer(k, dd)))

    forwards(3)
    for q in range(4):
        if TILES_AT == q:
            tiles_to_core()
            gain_to_plane()
        reduce_other(q)
        forwards(4 + q)
    if TILES_AT == 4:
        tiles_to_core()
        gain_to_plane()
    mine = d * 16 + x * 4
    for i in range(7):
        net.recv(gids[i], gc.at[i])
    for i in range(4):
        v = gp[mine + i]
        for k in range(7):
            v = v + gc[k, i]
        gy[y, i] = v
    gids = [net.send(gy.at[y], gy.at[y], y_peer(k)) for k in (1, 2, 3)]

    for lo, k in order:
        at = lax.rem(y + k, 4) * 8 + lo
        tile_grad(d * 32 + at, e, at, F32)
        net.recv(dc[lo, k], tiles4(dr, at))

        def join(q, _):
            v = e[at + q] + dr[at + q].astype(F32)
            if k:
                es[at + q] = v.astype(BF16)
            else:
                e[at + q] = v
            return 0

        lax.fori_loop(0, 4, join, 0)
        if k:
            ty[lo, k] = net.send(tiles4(es, at), yr.at[k - 1, pl.ds(lo, 4)], y_peer(k))

    for q in range(4):
        rs_own.append(scatter(h, 1, q))

    def ahead(b, acc):
        for u in range(4):
            i = b * 4 + u
            xs = x_all[:, sm[6, i]].reshape(256, 128)
            prod = jnp.dot(xs, w[sm[5, i]], preferred_element_type=F32)
            acc = acc * sm[7, i].astype(F32) + prod
            pf[i] = acc.astype(BF16)
        return acc

    lax.fori_loop(0, SLOTS // 4, ahead, jnp.zeros((256, 128), F32))
    for c in range(CT):
        v = pf[sm[8, c]].astype(F32) * sm[9, c].astype(F32)
        mx[:, c * 128 : (c + 1) * 128] = v.astype(BF16)
    mixed_out = pltpu.make_async_copy(mx, mixed_hbm, lsem.at[5])
    mixed_out.start()

    for k in (1, 2, 3):
        net.recv(gids[k - 1], gy.at[lax.rem(y + 4 - k, 4)])
    for i in range(4):
        gz[z, i] = gy[0, i] + gy[1, i] + gy[2, i] + gy[3, i]
    gids = [net.send(gz.at[z], gz.at[z], z_peer(k)) for k in range(1, 16)]

    def sum_y(q):
        v = e[y * 8 + q] + yr[0, q].astype(F32)
        return v + yr[1, q].astype(F32) + yr[2, q].astype(F32)

    for k in (1, 2, 3):
        net.recv(ty[4, k], yr.at[k - 1, pl.ds(4, 4)])
    for q in range(4, 8):
        fs[q] = sum_y(q).astype(BF16)
    tz1 = net.send(fs.at[pl.ds(4, 4)], fr.at[pl.ds(4, 4)], z1)
    for k in (1, 2, 3):
        net.recv(ty[0, k], yr.at[k - 1, pl.ds(0, 4)])
    for q in range(4):
        fa[q] = sum_y(q)

    net.recv(tz1, fr.at[pl.ds(4, 4)])
    for q in (2, 3):
        fs[q] = (fa[q] + fr[q + 4].astype(F32)).astype(BF16)
    tz2 = net.send(fs.at[pl.ds(2, 2)], fr.at[pl.ds(2, 2)], z2)
    for q in (0, 1):
        fa[q] = fa[q] + fr[q + 4].astype(F32)

    for k in (1, 2, 3):
        for q in range(4):
            net.recv(rs_own[q][k - 1], r.at[1, k - 1, pl.ds(q * 8, 8)])

    def own(rt, _):
        v = s[t, rt].astype(F32) + r[1, 0, rt].astype(F32)
        ig[rt] = v + r[1, 1, rt].astype(F32) + r[1, 2, rt].astype(F32)
        return 0

    lax.fori_loop(0, RT, own, 0)

    net.recv(tz2, fr.at[pl.ds(2, 2)])
    fs[1] = (fa[1] + fr[3].astype(F32)).astype(BF16)
    tz3 = net.send(fs.at[pl.ds(1, 1)], fr.at[pl.ds(1, 1)], z4)
    fa[0] = fa[0] + fr[2].astype(F32)

    for k in range(1, 16):
        net.recv(gids[k - 1], gz.at[lax.rem(z + 16 - k, 16)])
    for i in range(4):
        v = gz[0, i]
        for k in range(1, 16):
            v = v + gz[k, i]
        ga[mine + i] = v / gain[pl.ds(mine + i, 1), :]
    gids = [net.send(ga.at[pl.ds(mine, 4)], ga.at[pl.ds(mine, 4)], x_peer(k, dd)) for dd, k in plane]

    def hidden(rt, a):
        v = (ig[rt] + zr[rt].astype(F32)) * gain[pl.ds(rt, 1), :]
        ig[rt] = v
        return a + v * scaled[rt]

    acc = jnp.zeros((32, 128), F32)
    for q in range(4):
        net.recv(zids[q], zr.at[pl.ds(q * 8, 8)])
        acc = lax.fori_loop(q * 8, q * 8 + 8, hidden, acc)
    mean = jnp.sum(acc, axis=1, keepdims=True) * (1.0 / 4096.0)

    def finish(i, _):
        for u in range(4):
            rt = i * 4 + u
            v = inv[...] * (ig[rt] - scaled[rt] * mean)
            ox[:, lanes(rt)] = v.astype(BF16)
        return 0

    lax.fori_loop(0, RT // 4, finish, 0)
    gx_out = pltpu.make_async_copy(ox, gx_hbm, lsem.at[6])
    gx_out.start()

    net.recv(tz3, fr.at[pl.ds(1, 1)])
    keep = jnp.where(counts_s[0, f] > d, 1.0, 0.0)
    tiles[d] = (fa[0] + fr[1].astype(F32)).T * keep
    tc = net.send(tiles.at[d], tiles.at[d], core)

    for i, (dd, k) in enumerate(plane):
        net.recv(gids[i], ga.at[pl.ds(piece(dd, 4 - k), 4)])
    gg_out = pltpu.make_async_copy(ga, gg_hbm, lsem.at[8])
    gg_out.start()
    net.recv(tc, tiles.at[1 - d])
    gt_out = pltpu.make_async_copy(tiles, gt_hbm, lsem.at[7])
    gt_out.start()
    for copy in net.sent:
        copy.wait_send()
    for copy in (mixed_out, gx_out, gt_out, gg_out):
        copy.wait()


def outward(*refs):
    made, outs, held, (sem_in, sem_out) = refs[:4], refs[4:8], refs[8:12], refs[12:]
    into = [pltpu.make_async_copy(a, v, sem_in.at[i]) for i, (a, v) in enumerate(zip(made, held))]
    out = [pltpu.make_async_copy(v, o, sem_out.at[i]) for i, (v, o) in enumerate(zip(held, outs))]
    for c in into:
        c.start()
    for c, o in zip(into, out):
        c.wait()
        o.start()
    for o in out:
        o.wait()


def per_device(tokens, norm_gain, tile_values, tile_rows, tile_cols, tile_counts, grad_out):
    hbm = pl.BlockSpec(memory_space=pl.ANY)
    vmem = pl.BlockSpec(memory_space=pltpu.VMEM)
    smem = pl.BlockSpec(memory_space=pltpu.SMEM)
    rows8 = (8, RT, 32, 128)
    local = (RT, 32, 128)
    tiles32 = (32, 128, 128)
    shapes = (
        jax.ShapeDtypeStruct((256, 1792), BF16),
        jax.ShapeDtypeStruct((32, 4096), BF16),
        jax.ShapeDtypeStruct((RT, 1, 128), F32),
        jax.ShapeDtypeStruct((2, 128, 128), F32),
    )
    made = pl.pallas_call(
        kernel,
        out_shape=shapes,
        in_specs=[hbm, vmem, hbm, vmem, vmem, vmem, smem, hbm],
        out_specs=(hbm, hbm, hbm, hbm),
        scratch_shapes=[
            pltpu.VMEM((32, 4096), BF16),
            pltpu.VMEM((256, 1792), BF16),
            pltpu.VMEM((CT, 256, 128), BF16),
            pltpu.VMEM((CT, 128, 256), BF16),
            pltpu.VMEM(rows8, BF16),
            pltpu.VMEM(local, F32),
            pltpu.VMEM((32, 128), F32),
            pltpu.VMEM((SLOTS, 128, 128), BF16),
            pltpu.VMEM((SLOTS, 256, 128), BF16),
            pltpu.VMEM((SLOTS, 256, 128), BF16),
            pltpu.VMEM(rows8, BF16),
            pltpu.VMEM((2, 3) + local, BF16),
            pltpu.VMEM(local, BF16),
            pltpu.VMEM(local, BF16),
            pltpu.VMEM(local, F32),
            pltpu.VMEM(tiles32, BF16),
            pltpu.VMEM(tiles32, BF16),
            pltpu.VMEM(tiles32, F32),
            pltpu.VMEM(tiles32, BF16),
            pltpu.VMEM((3, 8, 128, 128), BF16),
            pltpu.VMEM((8, 128, 128), BF16),
            pltpu.VMEM((4, 128, 128), F32),
            pltpu.VMEM((8, 128, 128), BF16),
            pltpu.VMEM((2, 128, 128), F32),
            pltpu.VMEM((256, 1792), BF16),
            pltpu.VMEM((32, 4096), BF16),
            pltpu.VMEM((16, 128), jnp.int32),
            pltpu.SMEM((16, 128), jnp.int32),
            pltpu.VMEM((RT, 1, 128), F32),
            pltpu.VMEM((7, 4, 1, 128), F32),
            pltpu.VMEM((4, 4, 1, 128), F32),
            pltpu.VMEM((16, 4, 1, 128), F32),
            pltpu.VMEM((RT, 1, 128), F32),
            pltpu.SemaphoreType.DMA((NSEM,)),
            pltpu.SemaphoreType.DMA((NSEM,)),
            pltpu.SemaphoreType.DMA((9,)),
        ],
        compiler_params=pltpu.CompilerParams(
            collective_id=0, has_side_effects=True, vmem_limit_bytes=62 * 1024 * 1024
        ),
        name="sparse_mlp",
    )(
        tokens, norm_gain.reshape(RT, 128), tile_values, tile_rows, tile_cols, tile_counts,
        tile_counts, grad_out,
    )
    mixed, grad_x, grad_gain, grad_tiles = pl.pallas_call(
        outward,
        out_shape=shapes,
        in_specs=[hbm] * 4,
        out_specs=(hbm,) * 4,
        scratch_shapes=[pltpu.VMEM(a.shape, a.dtype) for a in shapes] + [pltpu.SemaphoreType.DMA((4,))] * 2,
        name="outward",
    )(*made)
    return mixed, grad_x, grad_gain.reshape(4096), grad_tiles


def solution(mesh):
    placed = (
        P(("dp", "fsdp", "tensor"), None),
        P(),
        P(("fsdp", "tensor"), None, None),
        P("tensor", None),
        P("tensor", None),
        P("tensor", None),
        P(("dp", "fsdp"), "tensor"),
    )
    return jax.shard_map(
        per_device,
        mesh=mesh,
        in_specs=placed,
        out_specs=(
            P(("dp", "fsdp"), "tensor"),
            P(("dp", "fsdp", "tensor"), None),
            P(),
            P(("fsdp", "tensor"), None, None),
        ),
        check_vma=False,
    )
```

```python
import functools

import jax
import jax.numpy as jnp
from jax import lax
from jax.experimental import pallas as pl
from jax.experimental.pallas import tpu as pltpu
from jax.sharding import PartitionSpec as P

MESH = pl.DeviceIdType.MESH
F32 = jnp.float32
BF16 = jnp.bfloat16
RT = 32
CT = 14
SLOTS = 64
NSEM = 160
X_OVER = (1, 2, 3, 3)
FORWARD = (0, 1, 2, 3)
NORM_FIRST = True
OWN_AT = (4, 4, 4, 4)
TILES_AT = 2


class Net:
    def __init__(self, ssem, rsem, anyone):
        self.ssem, self.rsem, self.anyone = ssem, rsem, anyone
        self.sent = []

    def send(self, src, dst, device):
        i = len(self.sent)
        copy = pltpu.make_async_remote_copy(
            src_ref=src,
            dst_ref=dst,
            send_sem=self.ssem.at[i],
            recv_sem=self.rsem.at[i],
            device_id=device,
            device_id_type=MESH,
        )
        copy.start()
        self.sent.append(copy)
        return i

    def recv(self, i, ref):
        pltpu.make_async_remote_copy(
            src_ref=ref,
            dst_ref=ref,
            send_sem=self.ssem.at[i],
            recv_sem=self.rsem.at[i],
            device_id=self.anyone,
            device_id_type=MESH,
        ).wait_recv()


def lanes(i):
    return pl.ds(pl.multiple_of(i * 128, 128), 128)


def slot_tables(rows, cols, counts, zl, table):
    sub = lax.broadcasted_iota(jnp.int32, (SLOTS, SLOTS), 0)
    lane = lax.broadcasted_iota(jnp.int32, (SLOTS, SLOTS), 1)
    wide = lax.broadcasted_iota(jnp.int32, (SLOTS, 128), 1)
    slot = lax.broadcasted_iota(jnp.int32, (SLOTS, 1), 0)

    def over_lanes(mask, value):
        return jnp.sum(jnp.where(mask, value, 0), axis=1, keepdims=True)

    def over_slots(mask, value):
        return jnp.sum(jnp.where(mask, value, 0), axis=0, keepdims=True)

    def row(column_vector):
        return over_slots(sub == lane, column_vector)

    def put(k, vector):
        table[pl.ds(k, 1), :] = vector

    table[...] = jnp.zeros_like(table)
    row_of, col_of = over_lanes(sub == lane, rows), over_lanes(sub == lane, cols)
    shard = lax.broadcasted_iota(jnp.int32, (SLOTS, 32), 0) >> 1
    shard_lane = lax.broadcasted_iota(jnp.int32, (SLOTS, 32), 1)
    count = over_lanes(shard == shard_lane, counts)
    j = slot & 1
    held = count > j
    apart = ((slot >> 1) & 7) ^ zl
    place = ((apart & 1) << 2) | (apart & 2) | (apart >> 2)
    stored = j * 32 + (slot >> 4) * 8 + place
    for base, key, other in ((0, row_of, col_of), (5, col_of, row_of)):
        key = jnp.where(held, key, 64)
        order = key * 64 + slot
        rank = over_lanes(row(order) < order, 1)
        same = over_lanes((row(key) == key) & (lane < sub), 1)
        at = rank == wide
        for k, vector in ((0, stored), (1, other), (2, jnp.minimum(same, 1))):
            put(base + k, over_slots(at, vector))
        put(base + 3, jnp.maximum(over_slots(key <= wide, 1) - 1, 0))
        put(base + 4, jnp.minimum(over_slots(key == wide, 1), 1))
    at = stored == wide
    put(10, over_slots(at, row_of))
    put(11, over_slots(at, col_of))


def kernel(
    tok_hbm, gain, tv_hbm, rows, cols, counts, counts_s, go_hbm,
    mixed_hbm, gx_hbm, gg_hbm, gt_hbm,
    tok, go, gs, gt, x_all, scaled, inv, w, pb, pf, s, r, zs, zr, ig,
    dt, dr, e, es, yr, fs, fa, fr, tiles, mx, ox, table, sm,
    gp, gc, gy, gz, ga, ssem, rsem, lsem,
):
    d, f, t = lax.axis_index("dp"), lax.axis_index("fsdp"), lax.axis_index("tensor")
    h, x, y, zl = t // 4, lax.rem(t, 4), f // 8, lax.rem(f, 8)
    z = h * 8 + zl
    core = {"dp": 1 - d}
    oc = lax.rem(t + 4, 8)
    other_half = {"tensor": oc}

    def x_peer(k, dd=0):
        peer = {"tensor": h * 4 + lax.rem(x + k, 4)}
        return {**peer, "dp": 1 - d} if dd else peer

    def y_peer(k):
        return {"fsdp": lax.rem(y + k, 4) * 8 + zl}

    def z_peer(k):
        to = lax.rem(z + k, 16)
        return {"fsdp": y * 8 + lax.rem(to, 8), "tensor": (to // 8) * 4 + x}

    z4 = {"fsdp": y * 8 + lax.rem(zl + 4, 8)}
    z2 = {"fsdp": f + 2 - 4 * lax.rem(zl // 2, 2)}
    z1 = {"fsdp": f + 1 - 2 * lax.rem(zl, 2)}
    plane = [(dd, k) for dd in (0, 1) for k in range(4) if dd or k]
    partners = [x_peer(k, dd) for dd, k in plane]
    partners += [y_peer(k) for k in (1, 2, 3)] + [z_peer(k) for k in range(1, 16)]

    own_w = d * 32 + y * 8
    other_w = (1 - d) * 32

    loads = [
        pltpu.make_async_copy(tok_hbm, tok, lsem.at[0]),
        pltpu.make_async_copy(tv_hbm.at[0], w.at[y * 8], lsem.at[1]),
        pltpu.make_async_copy(tv_hbm.at[1], w.at[32 + y * 8], lsem.at[2]),
        pltpu.make_async_copy(go_hbm, go, lsem.at[3]),
    ]
    for c in loads:
        c.start()
    barrier = pltpu.get_barrier_semaphore()
    for p in partners:
        pl.semaphore_signal(barrier, inc=1, device_id=p, device_id_type=MESH)

    def square(i, a):
        for u in range(4):
            v = tok[:, lanes(i * 4 + u)].astype(F32)
            a = a + v * v
        return a

    def norm(i, _):
        for u in range(4):
            rt = i * 4 + u
            v = tok[:, lanes(rt)].astype(F32) * inv[...]
            scaled[rt] = v
            x_all[t, rt] = (v * gain[pl.ds(rt, 1), :]).astype(BF16)
        return 0

    loads[0].wait()
    total = lax.fori_loop(0, RT // 4, square, jnp.zeros((32, 128), F32))
    inv_rms = lax.rsqrt(jnp.sum(total, axis=1, keepdims=True) * (1.0 / 4096.0) + 1e-05)
    inv[...] = jnp.broadcast_to(inv_rms, (32, 128))
    if NORM_FIRST:
        lax.fori_loop(0, RT // 4, norm, 0)
    loads[1].wait()
    loads[2].wait()
    pl.semaphore_wait(barrier, len(partners))

    net = Net(ssem, rsem, core)

    def w_at(base, lo, n):
        return w.at[pl.ds(base + lo, n)]

    def w_to_y(lo, n):
        return [net.send(w_at(own_w, lo, n), w_at(own_w, lo, n), y_peer(k)) for k in (1, 2, 3)]

    def x_chunk(c, q):
        return x_all.at[c, pl.ds(q * 8, 8)]

    xz, xfwd = [], []

    def x_over(q):
        xz.append(net.send(x_chunk(t, q), x_chunk(t, q), other_half))

    def forward(q):
        net.recv(xz[q], x_chunk(oc, q))
        xfwd.append([net.send(x_chunk(oc, q), x_chunk(oc, q), x_peer(k)) for k in (1, 2, 3)])

    def forwards(at):
        for q in range(4):
            if FORWARD[q] == at:
                forward(q)

    wz = [net.send(w_at(own_w, 0, 1), w_at(own_w, 1, 1), z4)]
    wy = [w_to_y(0, 1)]
    if not NORM_FIRST:
        lax.fori_loop(0, RT // 4, norm, 0)
    for q in range(4):
        if X_OVER[q] == 0:
            x_over(q)
    xown = [net.send(x_all.at[t], x_all.at[t], x_peer(k)) for k in (1, 2, 3)]

    net.recv(wz[0], w_at(own_w, 1, 1))
    wz.append(net.send(w_at(own_w, 0, 2), w_at(own_w, 2, 2), z2))
    wy.append(w_to_y(1, 1))
    for q in range(4):
        if X_OVER[q] == 1:
            x_over(q)

    net.recv(wz[1], w_at(own_w, 2, 2))
    wz.append(net.send(w_at(own_w, 0, 4), w_at(own_w, 4, 4), z1))
    wy.append(w_to_y(2, 2))
    for q in range(4):
        if X_OVER[q] == 2:
            x_over(q)

    net.recv(wz[2], w_at(own_w, 4, 4))
    wy.append(w_to_y(4, 4))
    wc = [net.send(w_at(own_w, 1, 7), w_at(own_w, 1, 7), core)]
    for q in range(4):
        if X_OVER[q] == 3:
            x_over(q)
    slot_tables(rows[...], cols[...], counts[...], zl, table)
    to_smem = pltpu.make_async_copy(table, sm, lsem.at[4])
    to_smem.start()
    loads[3].wait()
    for c in range(CT):
        v = go[:, c * 128 : (c + 1) * 128]
        gs[c] = v
        gt[c] = v.T
    forwards(0)
    for k in (1, 2, 3):
        base = d * 32 + lax.rem(y + 4 - k, 4) * 8
        for ids, (lo, n) in zip(wy, ((0, 1), (1, 1), (2, 2), (4, 4))):
            net.recv(ids[k - 1], w_at(base, lo, n))
        wc.append(net.send(w_at(base, 0, 8), w_at(base, 0, 8), core))
    forwards(1)
    net.recv(wc[0], w_at(other_w + y * 8, 1, 7))
    for k in (1, 2, 3):
        net.recv(wc[k], w_at(other_w + lax.rem(y + 4 - k, 4) * 8, 0, 8))
    to_smem.wait()
    forwards(2)

    def back(b, acc):
        for u in range(4):
            i = b * 4 + u
            prod = lax.dot_general(gs[sm[1, i]], w[sm[0, i]], (((1,), (1,)), ((), ())), preferred_element_type=F32)
            acc = acc * sm[2, i].astype(F32) + prod
            pb[i] = acc.astype(BF16)
        return acc

    lax.fori_loop(0, SLOTS // 4, back, jnp.zeros((256, 128), F32))
    rs_other, rs_own = [], []

    def assemble(q):
        def one(rt, _):
            v = pb[sm[3, rt]].astype(F32) * sm[4, rt].astype(F32)
            s[:, rt] = v.astype(BF16).reshape(8, 32, 128)
            return 0

        lax.fori_loop(q * 8, q * 8 + 8, one, 0)

    def scatter(half, slot, q):
        ids = []
        for k in (1, 2, 3):
            to = half * 4 + lax.rem(x + k, 4)
            ids.append(net.send(s.at[to, pl.ds(q * 8, 8)], r.at[slot, k - 1, pl.ds(q * 8, 8)], x_peer(k)))
        return ids

    for q in range(4):
        assemble(q)
        rs_other.append(scatter(1 - h, 0, q))

    zids = []

    def reduce_other(q):
        for k in (1, 2, 3):
            net.recv(rs_other[q][k - 1], r.at[0, k - 1, pl.ds(q * 8, 8)])

        def one(rt, _):
            v = s[oc, rt].astype(F32) + r[0, 0, rt].astype(F32)
            v = v + r[0, 1, rt].astype(F32) + r[0, 2, rt].astype(F32)
            zs[rt] = v.astype(BF16)
            return 0

        lax.fori_loop(q * 8, q * 8 + 8, one, 0)
        part = pl.ds(q * 8, 8)
        zids.append(net.send(zs.at[part], zr.at[part], other_half))

    def tile_grad(first, out, at, cast):
        def one(q, _):
            p = first + q
            xs = x_all[:, sm[10, p]].reshape(256, 128)
            out[at + q] = jnp.dot(gt[sm[11, p]], xs, preferred_element_type=F32).astype(cast)
            return 0

        lax.fori_loop(0, 4, one, 0, unroll=True)

    def tiles4(ref, at):
        return ref.at[pl.ds(at, 4)]

    order = [(lo, k) for lo in (4, 0) for k in (1, 2, 3, 0)]
    dc, ty = {}, {}

    def tiles_to_core():
        for k in (1, 2, 3):
            net.recv(xown[k - 1], x_all.at[h * 4 + lax.rem(x + 4 - k, 4)])
            for q in range(4):
                net.recv(xfwd[q][k - 1], x_chunk((1 - h) * 4 + lax.rem(x + 4 - k, 4), q))
        for lo, k in order:
            at = lax.rem(y + k, 4) * 8 + lo
            tile_grad(other_w + at, dt, at, BF16)
            dc[lo, k] = net.send(tiles4(dt, at), tiles4(dr, at), core)

    def gain_part(rt, _):
        v = s[:, rt].astype(F32) * x_all[:, rt].astype(F32)
        gp[rt] = jnp.sum(v.reshape(256, 128), axis=0, keepdims=True)
        return 0

    def piece(dd, k):
        return lax.rem(d + dd, 2) * 16 + lax.rem(x + k, 4) * 4

    gids = []

    def gain_to_plane():
        lax.fori_loop(0, RT, gain_part, 0)
        for i, (dd, k) in enumerate(plane):
            gids.append(net.send(gp.at[pl.ds(piece(dd, k), 4)], gc.at[i], x_peer(k, dd)))

    def own_sends(at):
        for q in range(4):
            if OWN_AT[q] == at:
                rs_own.append(scatter(h, 1, q))

    forwards(3)
    for q in range(4):
        if TILES_AT == q:
            tiles_to_core()
        reduce_other(q)
        forwards(4 + q)
        own_sends(q)
    if TILES_AT == 4:
        tiles_to_core()
    mine = d * 16 + x * 4

    for lo, k in order:
        at = lax.rem(y + k, 4) * 8 + lo
        tile_grad(d * 32 + at, e, at, F32)
        net.recv(dc[lo, k], tiles4(dr, at))

        def join(q, _):
            v = e[at + q] + dr[at + q].astype(F32)
            if k:
                es[at + q] = v.astype(BF16)
            else:
                e[at + q] = v
            return 0

        lax.fori_loop(0, 4, join, 0)
        if k:
            ty[lo, k] = net.send(tiles4(es, at), yr.at[k - 1, pl.ds(lo, 4)], y_peer(k))

    gain_to_plane()
    own_sends(4)

    def ahead(b, acc):
        for u in range(4):
            i = b * 4 + u
            xs = x_all[:, sm[6, i]].reshape(256, 128)
            prod = jnp.dot(xs, w[sm[5, i]], preferred_element_type=F32)
            acc = acc * sm[7, i].astype(F32) + prod
            pf[i] = acc.astype(BF16)
        return acc

    lax.fori_loop(0, SLOTS // 4, ahead, jnp.zeros((256, 128), F32))
    for c in range(CT):
        v = pf[sm[8, c]].astype(F32) * sm[9, c].astype(F32)
        mx[:, c * 128 : (c + 1) * 128] = v.astype(BF16)
    mixed_out = pltpu.make_async_copy(mx, mixed_hbm, lsem.at[5])
    mixed_out.start()

    for i in range(7):
        net.recv(gids[i], gc.at[i])
    for i in range(4):
        v = gp[mine + i]
        for k in range(7):
            v = v + gc[k, i]
        gy[y, i] = v
    gids = [net.send(gy.at[y], gy.at[y], y_peer(k)) for k in (1, 2, 3)]

    def sum_y(q):
        v = e[y * 8 + q] + yr[0, q].astype(F32)
        return v + yr[1, q].astype(F32) + yr[2, q].astype(F32)

    for k in (1, 2, 3):
        net.recv(ty[4, k], yr.at[k - 1, pl.ds(4, 4)])
    for q in range(4, 8):
        fs[q] = sum_y(q).astype(BF16)
    tz1 = net.send(fs.at[pl.ds(4, 4)], fr.at[pl.ds(4, 4)], z1)
    for k in (1, 2, 3):
        net.recv(ty[0, k], yr.at[k - 1, pl.ds(0, 4)])
    for q in range(4):
        fa[q] = sum_y(q)

    for k in (1, 2, 3):
        net.recv(gids[k - 1], gy.at[lax.rem(y + 4 - k, 4)])
    for i in range(4):
        gz[z, i] = gy[0, i] + gy[1, i] + gy[2, i] + gy[3, i]
    gids = [net.send(gz.at[z], gz.at[z], z_peer(k)) for k in range(1, 16)]

    net.recv(tz1, fr.at[pl.ds(4, 4)])
    for q in (2, 3):
        fs[q] = (fa[q] + fr[q + 4].astype(F32)).astype(BF16)
    tz2 = net.send(fs.at[pl.ds(2, 2)], fr.at[pl.ds(2, 2)], z2)
    for q in (0, 1):
        fa[q] = fa[q] + fr[q + 4].astype(F32)

    for k in (1, 2, 3):
        for q in range(4):
            net.recv(rs_own[q][k - 1], r.at[1, k - 1, pl.ds(q * 8, 8)])

    def own(rt, _):
        v = s[t, rt].astype(F32) + r[1, 0, rt].astype(F32)
        ig[rt] = v + r[1, 1, rt].astype(F32) + r[1, 2, rt].astype(F32)
        return 0

    lax.fori_loop(0, RT, own, 0)

    net.recv(tz2, fr.at[pl.ds(2, 2)])
    fs[1] = (fa[1] + fr[3].astype(F32)).astype(BF16)
    tz3 = net.send(fs.at[pl.ds(1, 1)], fr.at[pl.ds(1, 1)], z4)
    fa[0] = fa[0] + fr[2].astype(F32)

    for k in range(1, 16):
        net.recv(gids[k - 1], gz.at[lax.rem(z + 16 - k, 16)])
    for i in range(4):
        v = gz[0, i]
        for k in range(1, 16):
            v = v + gz[k, i]
        ga[mine + i] = v / gain[pl.ds(mine + i, 1), :]
    gids = [net.send(ga.at[pl.ds(mine, 4)], ga.at[pl.ds(mine, 4)], x_peer(k, dd)) for dd, k in plane]

    def hidden(rt, a):
        v = (ig[rt] + zr[rt].astype(F32)) * gain[pl.ds(rt, 1), :]
        ig[rt] = v
        return a + v * scaled[rt]

    acc = jnp.zeros((32, 128), F32)
    for q in range(4):
        net.recv(zids[q], zr.at[pl.ds(q * 8, 8)])
        acc = lax.fori_loop(q * 8, q * 8 + 8, hidden, acc)
    mean = jnp.sum(acc, axis=1, keepdims=True) * (1.0 / 4096.0)

    def finish(i, _):
        for u in range(4):
            rt = i * 4 + u
            v = inv[...] * (ig[rt] - scaled[rt] * mean)
            ox[:, lanes(rt)] = v.astype(BF16)
        return 0

    lax.fori_loop(0, RT // 4, finish, 0)
    gx_out = pltpu.make_async_copy(ox, gx_hbm, lsem.at[6])
    gx_out.start()

    net.recv(tz3, fr.at[pl.ds(1, 1)])
    keep = jnp.where(counts_s[0, f] > d, 1.0, 0.0)
    tiles[d] = (fa[0] + fr[1].astype(F32)).T * keep
    tc = net.send(tiles.at[d], tiles.at[d], core)

    for i, (dd, k) in enumerate(plane):
        net.recv(gids[i], ga.at[pl.ds(piece(dd, 4 - k), 4)])
    gg_out = pltpu.make_async_copy(ga, gg_hbm, lsem.at[8])
    gg_out.start()
    net.recv(tc, tiles.at[1 - d])
    gt_out = pltpu.make_async_copy(tiles, gt_hbm, lsem.at[7])
    gt_out.start()
    for copy in net.sent:
        copy.wait_send()
    for copy in (mixed_out, gx_out, gt_out, gg_out):
        copy.wait()


def outward(*refs):
    made, outs, held, (sem_in, sem_out) = refs[:4], refs[4:8], refs[8:12], refs[12:]
    into = [pltpu.make_async_copy(a, v, sem_in.at[i]) for i, (a, v) in enumerate(zip(made, held))]
    out = [pltpu.make_async_copy(v, o, sem_out.at[i]) for i, (v, o) in enumerate(zip(held, outs))]
    for c in into:
        c.start()
    for c, o in zip(into, out):
        c.wait()
        o.start()
    for o in out:
        o.wait()


def per_device(tokens, norm_gain, tile_values, tile_rows, tile_cols, tile_counts, grad_out):
    hbm = pl.BlockSpec(memory_space=pl.ANY)
    vmem = pl.BlockSpec(memory_space=pltpu.VMEM)
    smem = pl.BlockSpec(memory_space=pltpu.SMEM)
    rows8 = (8, RT, 32, 128)
    local = (RT, 32, 128)
    tiles32 = (32, 128, 128)
    shapes = (
        jax.ShapeDtypeStruct((256, 1792), BF16),
        jax.ShapeDtypeStruct((32, 4096), BF16),
        jax.ShapeDtypeStruct((RT, 1, 128), F32),
        jax.ShapeDtypeStruct((2, 128, 128), F32),
    )
    made = pl.pallas_call(
        kernel,
        out_shape=shapes,
        in_specs=[hbm, vmem, hbm, vmem, vmem, vmem, smem, hbm],
        out_specs=(hbm, hbm, hbm, hbm),
        scratch_shapes=[
            pltpu.VMEM((32, 4096), BF16),
            pltpu.VMEM((256, 1792), BF16),
            pltpu.VMEM((CT, 256, 128), BF16),
            pltpu.VMEM((CT, 128, 256), BF16),
            pltpu.VMEM(rows8, BF16),
            pltpu.VMEM(local, F32),
            pltpu.VMEM((32, 128), F32),
            pltpu.VMEM((SLOTS, 128, 128), BF16),
            pltpu.VMEM((SLOTS, 256, 128), BF16),
            pltpu.VMEM((SLOTS, 256, 128), BF16),
            pltpu.VMEM(rows8, BF16),
            pltpu.VMEM((2, 3) + local, BF16),
            pltpu.VMEM(local, BF16),
            pltpu.VMEM(local, BF16),
            pltpu.VMEM(local, F32),
            pltpu.VMEM(tiles32, BF16),
            pltpu.VMEM(tiles32, BF16),
            pltpu.VMEM(tiles32, F32),
            pltpu.VMEM(tiles32, BF16),
            pltpu.VMEM((3, 8, 128, 128), BF16),
            pltpu.VMEM((8, 128, 128), BF16),
            pltpu.VMEM((4, 128, 128), F32),
            pltpu.VMEM((8, 128, 128), BF16),
            pltpu.VMEM((2, 128, 128), F32),
            pltpu.VMEM((256, 1792), BF16),
            pltpu.VMEM((32, 4096), BF16),
            pltpu.VMEM((16, 128), jnp.int32),
            pltpu.SMEM((16, 128), jnp.int32),
            pltpu.VMEM((RT, 1, 128), F32),
            pltpu.VMEM((7, 4, 1, 128), F32),
            pltpu.VMEM((4, 4, 1, 128), F32),
            pltpu.VMEM((16, 4, 1, 128), F32),
            pltpu.VMEM((RT, 1, 128), F32),
            pltpu.SemaphoreType.DMA((NSEM,)),
            pltpu.SemaphoreType.DMA((NSEM,)),
            pltpu.SemaphoreType.DMA((9,)),
        ],
        compiler_params=pltpu.CompilerParams(
            collective_id=0, has_side_effects=True, vmem_limit_bytes=62 * 1024 * 1024
        ),
        name="sparse_mlp",
    )(
        tokens, norm_gain.reshape(RT, 128), tile_values, tile_rows, tile_cols, tile_counts,
        tile_counts, grad_out,
    )
    mixed, grad_x, grad_gain, grad_tiles = pl.pallas_call(
        outward,
        out_shape=shapes,
        in_specs=[hbm] * 4,
        out_specs=(hbm,) * 4,
        scratch_shapes=[pltpu.VMEM(a.shape, a.dtype) for a in shapes] + [pltpu.SemaphoreType.DMA((4,))] * 2,
        name="outward",
    )(*made)
    return mixed, grad_x, grad_gain.reshape(4096), grad_tiles


def solution(mesh):
    placed = (
        P(("dp", "fsdp", "tensor"), None),
        P(),
        P(("fsdp", "tensor"), None, None),
        P("tensor", None),
        P("tensor", None),
        P("tensor", None),
        P(("dp", "fsdp"), "tensor"),
    )
    return jax.shard_map(
        per_device,
        mesh=mesh,
        in_specs=placed,
        out_specs=(
            P(("dp", "fsdp"), "tensor"),
            P(("dp", "fsdp", "tensor"), None),
            P(),
            P(("fsdp", "tensor"), None, None),
        ),
        check_vma=False,
    )
```

```python
import functools

import jax
import jax.numpy as jnp
from jax import lax
from jax.experimental import pallas as pl
from jax.experimental.pallas import tpu as pltpu
from jax.sharding import PartitionSpec as P

MESH = pl.DeviceIdType.MESH
F32 = jnp.float32
BF16 = jnp.bfloat16
RT = 32
CT = 14
SLOTS = 64
NSEM = 160
X_OVER = (1, 2, 3, 3)
FORWARD = (0, 1, 2, 3)
NORM_FIRST = True
OWN_AT = (4, 4, 4, 4)
TILES_AT = 2


class Net:
    def __init__(self, ssem, rsem, anyone):
        self.ssem, self.rsem, self.anyone = ssem, rsem, anyone
        self.sent = []

    def send(self, src, dst, device):
        i = len(self.sent)
        copy = pltpu.make_async_remote_copy(
            src_ref=src,
            dst_ref=dst,
            send_sem=self.ssem.at[i],
            recv_sem=self.rsem.at[i],
            device_id=device,
            device_id_type=MESH,
        )
        copy.start()
        self.sent.append(copy)
        return i

    def recv(self, i, ref):
        pltpu.make_async_remote_copy(
            src_ref=ref,
            dst_ref=ref,
            send_sem=self.ssem.at[i],
            recv_sem=self.rsem.at[i],
            device_id=self.anyone,
            device_id_type=MESH,
        ).wait_recv()


def lanes(i):
    return pl.ds(pl.multiple_of(i * 128, 128), 128)


def slot_tables(rows, cols, counts, zl, table):
    sub = lax.broadcasted_iota(jnp.int32, (SLOTS, SLOTS), 0)
    lane = lax.broadcasted_iota(jnp.int32, (SLOTS, SLOTS), 1)
    wide = lax.broadcasted_iota(jnp.int32, (SLOTS, 128), 1)
    slot = lax.broadcasted_iota(jnp.int32, (SLOTS, 1), 0)

    def over_lanes(mask, value):
        return jnp.sum(jnp.where(mask, value, 0), axis=1, keepdims=True)

    def over_slots(mask, value):
        return jnp.sum(jnp.where(mask, value, 0), axis=0, keepdims=True)

    def row(column_vector):
        return over_slots(sub == lane, column_vector)

    def put(k, vector):
        table[pl.ds(k, 1), :] = vector

    table[...] = jnp.zeros_like(table)
    row_of, col_of = over_lanes(sub == lane, rows), over_lanes(sub == lane, cols)
    shard = lax.broadcasted_iota(jnp.int32, (SLOTS, 32), 0) >> 1
    shard_lane = lax.broadcasted_iota(jnp.int32, (SLOTS, 32), 1)
    count = over_lanes(shard == shard_lane, counts)
    j = slot & 1
    held = count > j
    apart = ((slot >> 1) & 7) ^ zl
    place = ((apart & 1) << 2) | (apart & 2) | (apart >> 2)
    stored = j * 32 + (slot >> 4) * 8 + place
    for base, key, other in ((0, row_of, col_of), (5, col_of, row_of)):
        key = jnp.where(held, key, 64)
        order = key * 64 + slot
        rank = over_lanes(row(order) < order, 1)
        same = over_lanes((row(key) == key) & (lane < sub), 1)
        at = rank == wide
        for k, vector in ((0, stored), (1, other), (2, jnp.minimum(same, 1))):
            put(base + k, over_slots(at, vector))
        put(base + 3, jnp.maximum(over_slots(key <= wide, 1) - 1, 0))
        put(base + 4, jnp.minimum(over_slots(key == wide, 1), 1))
    at = stored == wide
    put(10, over_slots(at, row_of))
    put(11, over_slots(at, col_of))


def kernel(
    tok_hbm, gain, tv_hbm, rows, cols, counts, counts_s, go_hbm,
    mixed_hbm, gx_hbm, gg_hbm, gt_hbm,
    tok, go, gs, gt, x_all, scaled, inv, w, pb, pf, s, r, zs, zr, ig,
    dt, dr, e, es, yr, fs, fa, fr, tiles, mx, ox, table, sm,
    gp, gc, gy, gz, ga, ssem, rsem, lsem,
):
    d, f, t = lax.axis_index("dp"), lax.axis_index("fsdp"), lax.axis_index("tensor")
    h, x, y, zl = t // 4, lax.rem(t, 4), f // 8, lax.rem(f, 8)
    z = h * 8 + zl
    core = {"dp": 1 - d}
    oc = lax.rem(t + 4, 8)
    other_half = {"tensor": oc}

    def x_peer(k, dd=0):
        peer = {"tensor": h * 4 + lax.rem(x + k, 4)}
        return {**peer, "dp": 1 - d} if dd else peer

    def y_peer(k):
        return {"fsdp": lax.rem(y + k, 4) * 8 + zl}

    def z_peer(k):
        to = lax.rem(z + k, 16)
        return {"fsdp": y * 8 + lax.rem(to, 8), "tensor": (to // 8) * 4 + x}

    z4 = {"fsdp": y * 8 + lax.rem(zl + 4, 8)}
    z2 = {"fsdp": f + 2 - 4 * lax.rem(zl // 2, 2)}
    z1 = {"fsdp": f + 1 - 2 * lax.rem(zl, 2)}
    plane = [(dd, k) for dd in (0, 1) for k in range(4) if dd or k]
    partners = [x_peer(k, dd) for dd, k in plane]
    partners += [y_peer(k) for k in (1, 2, 3)] + [z_peer(k) for k in range(1, 16)]

    own_w = d * 32 + y * 8
    other_w = (1 - d) * 32

    loads = [
        pltpu.make_async_copy(tok_hbm, tok, lsem.at[0]),
        pltpu.make_async_copy(tv_hbm.at[0], w.at[y * 8], lsem.at[1]),
        pltpu.make_async_copy(tv_hbm.at[1], w.at[32 + y * 8], lsem.at[2]),
        pltpu.make_async_copy(go_hbm, go, lsem.at[3]),
    ]
    for c in loads:
        c.start()
    barrier = pltpu.get_barrier_semaphore()
    for p in partners:
        pl.semaphore_signal(barrier, inc=1, device_id=p, device_id_type=MESH)

    def square(i, a):
        for u in range(4):
            v = tok[:, lanes(i * 4 + u)].astype(F32)
            a = a + v * v
        return a

    def norm(i, _):
        for u in range(4):
            rt = i * 4 + u
            v = tok[:, lanes(rt)].astype(F32) * inv[...]
            scaled[rt] = v
            x_all[t, rt] = (v * gain[pl.ds(rt, 1), :]).astype(BF16)
        return 0

    loads[0].wait()
    total = lax.fori_loop(0, RT // 4, square, jnp.zeros((32, 128), F32))
    inv_rms = lax.rsqrt(jnp.sum(total, axis=1, keepdims=True) * (1.0 / 4096.0) + 1e-05)
    inv[...] = jnp.broadcast_to(inv_rms, (32, 128))
    if NORM_FIRST:
        lax.fori_loop(0, RT // 4, norm, 0)
    loads[1].wait()
    loads[2].wait()
    pl.semaphore_wait(barrier, len(partners))

    net = Net(ssem, rsem, core)

    def w_at(base, lo, n):
        return w.at[pl.ds(base + lo, n)]

    def w_to_y(lo, n):
        return [net.send(w_at(own_w, lo, n), w_at(own_w, lo, n), y_peer(k)) for k in (1, 2, 3)]

    def x_chunk(c, q):
        return x_all.at[c, pl.ds(q * 8, 8)]

    xz, xfwd = [], []

    def x_over(q):
        xz.append(net.send(x_chunk(t, q), x_chunk(t, q), other_half))

    def forward(q):
        net.recv(xz[q], x_chunk(oc, q))
        xfwd.append([net.send(x_chunk(oc, q), x_chunk(oc, q), x_peer(k)) for k in (1, 2, 3)])

    def forwards(at):
        for q in range(4):
            if FORWARD[q] == at:
                forward(q)

    wz = [net.send(w_at(own_w, 0, 1), w_at(own_w, 1, 1), z4)]
    wy = [w_to_y(0, 1)]
    if not NORM_FIRST:
        lax.fori_loop(0, RT // 4, norm, 0)
    for q in range(4):
        if X_OVER[q] == 0:
            x_over(q)
    xown = [net.send(x_all.at[t], x_all.at[t], x_peer(k)) for k in (1, 2, 3)]

    net.recv(wz[0], w_at(own_w, 1, 1))
    wz.append(net.send(w_at(own_w, 0, 2), w_at(own_w, 2, 2), z2))
    wy.append(w_to_y(1, 1))
    for q in range(4):
        if X_OVER[q] == 1:
            x_over(q)

    net.recv(wz[1], w_at(own_w, 2, 2))
    wz.append(net.send(w_at(own_w, 0, 4), w_at(own_w, 4, 4), z1))
    wy.append(w_to_y(2, 2))
    for q in range(4):
        if X_OVER[q] == 2:
            x_over(q)

    net.recv(wz[2], w_at(own_w, 4, 4))
    wy.append(w_to_y(4, 4))
    wc = [net.send(w_at(own_w, 1, 7), w_at(own_w, 1, 7), core)]
    for q in range(4):
        if X_OVER[q] == 3:
            x_over(q)
    slot_tables(rows[...], cols[...], counts[...], zl, table)
    to_smem = pltpu.make_async_copy(table, sm, lsem.at[4])
    to_smem.start()
    loads[3].wait()
    for c in range(CT):
        v = go[:, c * 128 : (c + 1) * 128]
        gs[c] = v
        gt[c] = v.T
    forwards(0)
    for k in (1, 2, 3):
        base = d * 32 + lax.rem(y + 4 - k, 4) * 8
        for ids, (lo, n) in zip(wy, ((0, 1), (1, 1), (2, 2), (4, 4))):
            net.recv(ids[k - 1], w_at(base, lo, n))
        wc.append(net.send(w_at(base, 0, 8), w_at(base, 0, 8), core))
    forwards(1)
    net.recv(wc[0], w_at(other_w + y * 8, 1, 7))
    for k in (1, 2, 3):
        net.recv(wc[k], w_at(other_w + lax.rem(y + 4 - k, 4) * 8, 0, 8))
    to_smem.wait()
    forwards(2)

    def back(b, acc):
        for u in range(4):
            i = b * 4 + u
            prod = lax.dot_general(gs[sm[1, i]], w[sm[0, i]], (((1,), (1,)), ((), ())), preferred_element_type=F32)
            acc = acc * sm[2, i].astype(F32) + prod
            pb[i] = acc.astype(BF16)
        return acc

    lax.fori_loop(0, SLOTS // 4, back, jnp.zeros((256, 128), F32))
    rs_other, rs_own = [], []

    def assemble(q):
        def one(rt, _):
            v = pb[sm[3, rt]].astype(F32) * sm[4, rt].astype(F32)
            s[:, rt] = v.astype(BF16).reshape(8, 32, 128)
            return 0

        lax.fori_loop(q * 8, q * 8 + 8, one, 0)

    def scatter(half, slot, q):
        ids = []
        for k in (1, 2, 3):
            to = half * 4 + lax.rem(x + k, 4)
            ids.append(net.send(s.at[to, pl.ds(q * 8, 8)], r.at[slot, k - 1, pl.ds(q * 8, 8)], x_peer(k)))
        return ids

    for q in range(4):
        assemble(q)
        rs_other.append(scatter(1 - h, 0, q))

    zids = []

    def reduce_other(q):
        for k in (1, 2, 3):
            net.recv(rs_other[q][k - 1], r.at[0, k - 1, pl.ds(q * 8, 8)])

        def one(rt, _):
            v = s[oc, rt].astype(F32) + r[0, 0, rt].astype(F32)
            v = v + r[0, 1, rt].astype(F32) + r[0, 2, rt].astype(F32)
            zs[rt] = v.astype(BF16)
            return 0

        lax.fori_loop(q * 8, q * 8 + 8, one, 0)
        part = pl.ds(q * 8, 8)
        zids.append(net.send(zs.at[part], zr.at[part], other_half))

    def tile_grad(first, out, at, cast):
        def one(q, _):
            p = first + q
            xs = x_all[:, sm[10, p]].reshape(256, 128)
            out[at + q] = jnp.dot(gt[sm[11, p]], xs, preferred_element_type=F32).astype(cast)
            return 0

        lax.fori_loop(0, 4, one, 0, unroll=True)

    def tiles4(ref, at):
        return ref.at[pl.ds(at, 4)]

    order = [(lo, k) for lo in (4, 0) for k in (1, 2, 3, 0)]
    dc, ty = {}, {}

    def tiles_to_core():
        for k in (1, 2, 3):
            net.recv(xown[k - 1], x_all.at[h * 4 + lax.rem(x + 4 - k, 4)])
            for q in range(4):
                net.recv(xfwd[q][k - 1], x_chunk((1 - h) * 4 + lax.rem(x + 4 - k, 4), q))
        for lo, k in order:
            at = lax.rem(y + k, 4) * 8 + lo
            tile_grad(other_w + at, dt, at, BF16)
            dc[lo, k] = net.send(tiles4(dt, at), tiles4(dr, at), core)

    def gain_part(rt, _):
        v = s[:, rt].astype(F32) * x_all[:, rt].astype(F32)
        gp[rt] = jnp.sum(v.reshape(256, 128), axis=0, keepdims=True)
        return 0

    def piece(dd, k):
        return lax.rem(d + dd, 2) * 16 + lax.rem(x + k, 4) * 4

    gids = []

    def gain_to_plane():
        lax.fori_loop(0, RT, gain_part, 0)
        for i, (dd, k) in enumerate(plane):
            gids.append(net.send(gp.at[pl.ds(piece(dd, k), 4)], gc.at[i], x_peer(k, dd)))

    def own_sends(at):
        for q in range(4):
            if OWN_AT[q] == at:
                rs_own.append(scatter(h, 1, q))

    forwards(3)
    for q in range(4):
        if TILES_AT == q:
            tiles_to_core()
        reduce_other(q)
        forwards(4 + q)
        own_sends(q)
    if TILES_AT == 4:
        tiles_to_core()
    mine = d * 16 + x * 4

    gain_to_plane()
    for lo, k in order:
        if (lo, k) == (0, 1):
            for i in range(7):
                net.recv(gids[i], gc.at[i])
            for i in range(4):
                v = gp[mine + i]
                for n in range(7):
                    v = v + gc[n, i]
                gy[y, i] = v
            gids = [net.send(gy.at[y], gy.at[y], y_peer(n)) for n in (1, 2, 3)]
        at = lax.rem(y + k, 4) * 8 + lo
        tile_grad(d * 32 + at, e, at, F32)
        net.recv(dc[lo, k], tiles4(dr, at))

        def join(q, _):
            v = e[at + q] + dr[at + q].astype(F32)
            if k:
                es[at + q] = v.astype(BF16)
            else:
                e[at + q] = v
            return 0

        lax.fori_loop(0, 4, join, 0)
        if k:
            ty[lo, k] = net.send(tiles4(es, at), yr.at[k - 1, pl.ds(lo, 4)], y_peer(k))

    own_sends(4)

    def ahead(b, acc):
        for u in range(4):
            i = b * 4 + u
            xs = x_all[:, sm[6, i]].reshape(256, 128)
            prod = jnp.dot(xs, w[sm[5, i]], preferred_element_type=F32)
            acc = acc * sm[7, i].astype(F32) + prod
            pf[i] = acc.astype(BF16)
        return acc

    lax.fori_loop(0, SLOTS // 4, ahead, jnp.zeros((256, 128), F32))
    for c in range(CT):
        v = pf[sm[8, c]].astype(F32) * sm[9, c].astype(F32)
        mx[:, c * 128 : (c + 1) * 128] = v.astype(BF16)
    mixed_out = pltpu.make_async_copy(mx, mixed_hbm, lsem.at[5])
    mixed_out.start()


    for k in (1, 2, 3):
        net.recv(gids[k - 1], gy.at[lax.rem(y + 4 - k, 4)])
    for i in range(4):
        gz[z, i] = gy[0, i] + gy[1, i] + gy[2, i] + gy[3, i]
    gids = [net.send(gz.at[z], gz.at[z], z_peer(k)) for k in range(1, 16)]

    def sum_y(q):
        v = e[y * 8 + q] + yr[0, q].astype(F32)
        return v + yr[1, q].astype(F32) + yr[2, q].astype(F32)

    for k in (1, 2, 3):
        net.recv(ty[4, k], yr.at[k - 1, pl.ds(4, 4)])
    for q in range(4, 8):
        fs[q] = sum_y(q).astype(BF16)
    tz1 = net.send(fs.at[pl.ds(4, 4)], fr.at[pl.ds(4, 4)], z1)
    for k in (1, 2, 3):
        net.recv(ty[0, k], yr.at[k - 1, pl.ds(0, 4)])
    for q in range(4):
        fa[q] = sum_y(q)

    net.recv(tz1, fr.at[pl.ds(4, 4)])
    for q in (2, 3):
        fs[q] = (fa[q] + fr[q + 4].astype(F32)).astype(BF16)
    tz2 = net.send(fs.at[pl.ds(2, 2)], fr.at[pl.ds(2, 2)], z2)
    for q in (0, 1):
        fa[q] = fa[q] + fr[q + 4].astype(F32)

    for k in (1, 2, 3):
        for q in range(4):
            net.recv(rs_own[q][k - 1], r.at[1, k - 1, pl.ds(q * 8, 8)])

    def own(rt, _):
        v = s[t, rt].astype(F32) + r[1, 0, rt].astype(F32)
        ig[rt] = v + r[1, 1, rt].astype(F32) + r[1, 2, rt].astype(F32)
        return 0

    lax.fori_loop(0, RT, own, 0)

    net.recv(tz2, fr.at[pl.ds(2, 2)])
    fs[1] = (fa[1] + fr[3].astype(F32)).astype(BF16)
    tz3 = net.send(fs.at[pl.ds(1, 1)], fr.at[pl.ds(1, 1)], z4)
    fa[0] = fa[0] + fr[2].astype(F32)

    for k in range(1, 16):
        net.recv(gids[k - 1], gz.at[lax.rem(z + 16 - k, 16)])
    for i in range(4):
        v = gz[0, i]
        for k in range(1, 16):
            v = v + gz[k, i]
        ga[mine + i] = v / gain[pl.ds(mine + i, 1), :]
    gids = [net.send(ga.at[pl.ds(mine, 4)], ga.at[pl.ds(mine, 4)], x_peer(k, dd)) for dd, k in plane]

    def hidden(rt, a):
        v = (ig[rt] + zr[rt].astype(F32)) * gain[pl.ds(rt, 1), :]
        ig[rt] = v
        return a + v * scaled[rt]

    acc = jnp.zeros((32, 128), F32)
    for q in range(4):
        net.recv(zids[q], zr.at[pl.ds(q * 8, 8)])
        acc = lax.fori_loop(q * 8, q * 8 + 8, hidden, acc)
    mean = jnp.sum(acc, axis=1, keepdims=True) * (1.0 / 4096.0)

    def finish(i, _):
        for u in range(4):
            rt = i * 4 + u
            v = inv[...] * (ig[rt] - scaled[rt] * mean)
            ox[:, lanes(rt)] = v.astype(BF16)
        return 0

    lax.fori_loop(0, RT // 4, finish, 0)
    gx_out = pltpu.make_async_copy(ox, gx_hbm, lsem.at[6])
    gx_out.start()

    net.recv(tz3, fr.at[pl.ds(1, 1)])
    keep = jnp.where(counts_s[0, f] > d, 1.0, 0.0)
    tiles[d] = (fa[0] + fr[1].astype(F32)).T * keep
    tc = net.send(tiles.at[d], tiles.at[d], core)

    for i, (dd, k) in enumerate(plane):
        net.recv(gids[i], ga.at[pl.ds(piece(dd, 4 - k), 4)])
    gg_out = pltpu.make_async_copy(ga, gg_hbm, lsem.at[8])
    gg_out.start()
    net.recv(tc, tiles.at[1 - d])
    gt_out = pltpu.make_async_copy(tiles, gt_hbm, lsem.at[7])
    gt_out.start()
    for copy in net.sent:
        copy.wait_send()
    for copy in (mixed_out, gx_out, gt_out, gg_out):
        copy.wait()


def outward(*refs):
    made, outs, held, (sem_in, sem_out) = refs[:4], refs[4:8], refs[8:12], refs[12:]
    into = [pltpu.make_async_copy(a, v, sem_in.at[i]) for i, (a, v) in enumerate(zip(made, held))]
    out = [pltpu.make_async_copy(v, o, sem_out.at[i]) for i, (v, o) in enumerate(zip(held, outs))]
    for c in into:
        c.start()
    for c, o in zip(into, out):
        c.wait()
        o.start()
    for o in out:
        o.wait()


def per_device(tokens, norm_gain, tile_values, tile_rows, tile_cols, tile_counts, grad_out):
    hbm = pl.BlockSpec(memory_space=pl.ANY)
    vmem = pl.BlockSpec(memory_space=pltpu.VMEM)
    smem = pl.BlockSpec(memory_space=pltpu.SMEM)
    rows8 = (8, RT, 32, 128)
    local = (RT, 32, 128)
    tiles32 = (32, 128, 128)
    shapes = (
        jax.ShapeDtypeStruct((256, 1792), BF16),
        jax.ShapeDtypeStruct((32, 4096), BF16),
        jax.ShapeDtypeStruct((RT, 1, 128), F32),
        jax.ShapeDtypeStruct((2, 128, 128), F32),
    )
    made = pl.pallas_call(
        kernel,
        out_shape=shapes,
        in_specs=[hbm, vmem, hbm, vmem, vmem, vmem, smem, hbm],
        out_specs=(hbm, hbm, hbm, hbm),
        scratch_shapes=[
            pltpu.VMEM((32, 4096), BF16),
            pltpu.VMEM((256, 1792), BF16),
            pltpu.VMEM((CT, 256, 128), BF16),
            pltpu.VMEM((CT, 128, 256), BF16),
            pltpu.VMEM(rows8, BF16),
            pltpu.VMEM(local, F32),
            pltpu.VMEM((32, 128), F32),
            pltpu.VMEM((SLOTS, 128, 128), BF16),
            pltpu.VMEM((SLOTS, 256, 128), BF16),
            pltpu.VMEM((SLOTS, 256, 128), BF16),
            pltpu.VMEM(rows8, BF16),
            pltpu.VMEM((2, 3) + local, BF16),
            pltpu.VMEM(local, BF16),
            pltpu.VMEM(local, BF16),
            pltpu.VMEM(local, F32),
            pltpu.VMEM(tiles32, BF16),
            pltpu.VMEM(tiles32, BF16),
            pltpu.VMEM(tiles32, F32),
            pltpu.VMEM(tiles32, BF16),
            pltpu.VMEM((3, 8, 128, 128), BF16),
            pltpu.VMEM((8, 128, 128), BF16),
            pltpu.VMEM((4, 128, 128), F32),
            pltpu.VMEM((8, 128, 128), BF16),
            pltpu.VMEM((2, 128, 128), F32),
            pltpu.VMEM((256, 1792), BF16),
            pltpu.VMEM((32, 4096), BF16),
            pltpu.VMEM((16, 128), jnp.int32),
            pltpu.SMEM((16, 128), jnp.int32),
            pltpu.VMEM((RT, 1, 128), F32),
            pltpu.VMEM((7, 4, 1, 128), F32),
            pltpu.VMEM((4, 4, 1, 128), F32),
            pltpu.VMEM((16, 4, 1, 128), F32),
            pltpu.VMEM((RT, 1, 128), F32),
            pltpu.SemaphoreType.DMA((NSEM,)),
            pltpu.SemaphoreType.DMA((NSEM,)),
            pltpu.SemaphoreType.DMA((9,)),
        ],
        compiler_params=pltpu.CompilerParams(
            collective_id=0, has_side_effects=True, vmem_limit_bytes=62 * 1024 * 1024
        ),
        name="sparse_mlp",
    )(
        tokens, norm_gain.reshape(RT, 128), tile_values, tile_rows, tile_cols, tile_counts,
        tile_counts, grad_out,
    )
    mixed, grad_x, grad_gain, grad_tiles = pl.pallas_call(
        outward,
        out_shape=shapes,
        in_specs=[hbm] * 4,
        out_specs=(hbm,) * 4,
        scratch_shapes=[pltpu.VMEM(a.shape, a.dtype) for a in shapes] + [pltpu.SemaphoreType.DMA((4,))] * 2,
        name="outward",
    )(*made)
    return mixed, grad_x, grad_gain.reshape(4096), grad_tiles


def solution(mesh):
    placed = (
        P(("dp", "fsdp", "tensor"), None),
        P(),
        P(("fsdp", "tensor"), None, None),
        P("tensor", None),
        P("tensor", None),
        P("tensor", None),
        P(("dp", "fsdp"), "tensor"),
    )
    return jax.shard_map(
        per_device,
        mesh=mesh,
        in_specs=placed,
        out_specs=(
            P(("dp", "fsdp"), "tensor"),
            P(("dp", "fsdp", "tensor"), None),
            P(),
            P(("fsdp", "tensor"), None, None),
        ),
        check_vma=False,
    )
```
